32 devices in a mesh: groups: 2 (over y), gx: 4 (over z), gy: 2 (over x), gz: 2 (over core).
Axes of the slice: x: 2, y: 2, z: 4, core: 2. Of those that a mesh axis runs over, the one named last changes fastest.
Arguments:
- adjoint_source: float32 [5, 4, 4, 4, 8, 2, 256], P(None, None, None, None, ('groups', 'gx'), 'gy', 'gz'), parts along dimension 4, may hold values from -6 to 6
- diagonal: bfloat16 [5, 4, 4, 4, 8, 2, 256], P(None, None, None, None, ('groups', 'gx'), 'gy', 'gz'), parts along dimension 4, may hold values from 2 to 4
- volume_coupling: bfloat16 [3, 5, 5, 4, 4, 4, 8, 2, 256], P(None, None, None, None, None, None, ('groups', 'gx'), 'gy', 'gz'), parts along dimension 6, may hold values from -0.5 to 0.5
- surface_coupling: bfloat16 [6, 5, 5, 4, 4, 8, 2, 256], P(None, None, None, None, None, ('groups', 'gx'), 'gy', 'gz'), parts along dimension 5, may hold values from -1.1953125 to 1.1953125
- mortar_owner: int32 [2048, 1], P(('groups', 'gx', 'gy', 'gz')), parts along dimension 0, may hold values from 0 to 3, as said below
- mortar_fine: int32 [2048], P(('groups', 'gx', 'gy', 'gz')), parts along dimension 0, may hold values from 0 to 127, as said below
- mortar_coarse: int32 [2048], P(('groups', 'gx', 'gy', 'gz')), parts along dimension 0, may hold values from 0 to 127, as said below
- mortar_quarter: int32 [2048], P(('groups', 'gx', 'gy', 'gz')), parts along dimension 0, may hold values from 0 to 3
- mortar_side: int32 [2048], P(('groups', 'gx', 'gy', 'gz')), parts along dimension 0, may hold values from 0 to 5
- mortar_coupling: float32 [2048, 2, 5, 5], P(('groups', 'gx', 'gy', 'gz')), parts along dimension 0, may hold values from -2.4 to 2.4
Outputs:
- adjoint_field: float32 [5, 4, 4, 4, 8, 2, 256], P(None, None, None, None, ('groups', 'gx'), 'gy', 'gz'), parts along dimension 4
The draws below stay inside these ranges and needn't reach their ends.
There are 2 independent parts, one for each index of `groups`. The reference program is written for one: setup_inputs(seed, part) draws one part's arguments, and reference() takes and returns one part's arrays. A program takes and returns all parts, laid end to end along the dimension named above; each array names one. Nothing has to cross between parts.
Inputs may be any that keep to these rules, and one draw needn't show every extreme that they name: `mortar_owner`: the owner index of a row is the first-dimension index of the row's device or one beside it; within the rows of one device (aligned blocks of 64 rows) no owner index is named by more than 32 rows, and some owner index is named by exactly 32 rows. `mortar_fine`: where the owner is the device below along the first dimension, the fine element lies in the device's first element layer along that dimension and the face is 0; where it is the device above, in the last layer and the face is 1. `mortar_coarse`: where the owner differs from the row's device, the coarse element lies across the face from the fine element, in the owner's facing element layer.
All inputs are finite; a program needn't handle non-finite values.
Results may differ from the reference program's by a relative error of at most 0.0003.
Values sent between devices are 32-bit elements; how exact they have to be, the bound alone decides.
A program may use at most 64 MiB of HBM per device.

```python
import jax
import jax.numpy as jnp
import numpy as np
from jax import lax

VARS = 5
NODES = 4
CX = 1
CY = 1
CZ = 128
M_DEV = 64
KRYLOV = 4
CAP = 32
NX = 4
NY = 2
NZ = 256
HANG = 1024
N_GX = 4
N_GY = 2
N_GZ = 2


def mortar_layout(key):
    hang_rows = jnp.arange(HANG, dtype=jnp.int32)
    devices = HANG // M_DEV
    dev_x = hang_rows // M_DEV // (N_GY * N_GZ)
    first_index = jnp.arange(devices, dtype=jnp.int32) // (N_GY * N_GZ)
    primary = jax.random.randint(jax.random.fold_in(key, 101), (devices,), 0, 3).astype(jnp.int32) - 1
    primary = jnp.where((first_index + primary < 0) | (first_index + primary >= N_GX), 0, primary)
    device_keys = jax.random.split(jax.random.fold_in(key, 102), devices)
    ordering = jax.vmap(lambda single: jax.random.permutation(single, M_DEV))(device_keys).reshape(HANG)
    primary_row = primary[hang_rows // M_DEV]
    picked = jax.random.randint(jax.random.fold_in(key, 103), (HANG,), 0, 2)
    first_other = jnp.where(primary_row == -1, 0, -1)
    second_other = jnp.where(primary_row == 1, 0, 1)
    chosen = jnp.where(picked == 0, first_other, second_other)
    spare = jnp.where(picked == 0, second_other, first_other)
    chosen = jnp.where((dev_x + chosen < 0) | (dev_x + chosen >= N_GX), spare, chosen)
    offset = jnp.where(ordering < CAP, primary_row, chosen).astype(jnp.int32)
    owner = (dev_x + offset).astype(jnp.int32)
    fine_x = jax.random.randint(jax.random.fold_in(key, 104), (HANG,), 0, CX)
    fine_y = jax.random.randint(jax.random.fold_in(key, 105), (HANG,), 0, CY)
    fine_z = jax.random.randint(jax.random.fold_in(key, 106), (HANG,), 0, CZ)
    other_x = jax.random.randint(jax.random.fold_in(key, 107), (HANG,), 0, CX)
    other_y = jax.random.randint(jax.random.fold_in(key, 108), (HANG,), 0, CY)
    other_z = jax.random.randint(jax.random.fold_in(key, 109), (HANG,), 0, CZ)
    free_side = jax.random.randint(jax.random.fold_in(key, 110), (HANG,), 0, 6)
    fine_x = jnp.where(offset == 1, CX - 1, jnp.where(offset == -1, 0, fine_x))
    coarse_x = jnp.where(offset == 1, 0, jnp.where(offset == -1, CX - 1, other_x))
    coarse_y = jnp.where(offset == 0, other_y, fine_y)
    coarse_z = jnp.where(offset == 0, other_z, fine_z)
    side = jnp.where(offset == 1, 1, jnp.where(offset == -1, 0, free_side)).astype(jnp.int32)
    fine = ((fine_x * CY + fine_y) * CZ + fine_z).astype(jnp.int32)
    coarse = ((coarse_x * CY + coarse_y) * CZ + coarse_z).astype(jnp.int32)
    return (owner, fine, coarse, side)


def draw_mortar_owner(key, part):
    return mortar_layout(key)[0].reshape(HANG, 1)


def draw_mortar_fine(key, part):
    return mortar_layout(key)[1]


def draw_mortar_coarse(key, part):
    return mortar_layout(key)[2]


def draw_mortar_side(key, part):
    return mortar_layout(key)[3]


def set_ends(values, stream_key, least, high):
    shape = values.shape
    spot = [jax.random.randint(jax.random.fold_in(stream_key, axis), (), 0, shape[axis]) for axis in range(len(shape))]
    values = values.at[tuple(spot)].set(least)
    longest = shape.index(max(shape))
    spot[longest] = (spot[longest] + 1) % shape[longest]
    return values.at[tuple(spot)].set(high)


def level_of(stream_key, dims, pieces, low, top_value):
    loudness = 1.0
    for axis_at, parts in pieces:
        draws = jax.random.uniform(jax.random.fold_in(jax.random.fold_in(stream_key, 6), axis_at), (parts,), jnp.float32, low / len(pieces), top_value / len(pieces))
        loudness = loudness * jnp.repeat(jnp.exp(draws), dims[axis_at] // parts).reshape((-1,) + (1,) * (len(dims) - 1 - axis_at))
    return loudness


def scatter_about(rng, dims, deviation, limit, cuts=(), held_as=jnp.bfloat16):
    values = jax.random.normal(rng, dims, jnp.float32) * deviation
    if len(cuts) > 0:
        values = level_of(rng, dims, cuts, -0.22, 0.18) * values
    return jnp.clip(values, min=-limit, max=limit).astype(held_as)


def setup_inputs(seed: int = 0, part: int = 0) -> dict:
    keys = jax.random.split(jax.random.key(seed), 11)
    own_keys = jax.random.split(jax.random.fold_in(keys[10], part), 11)
    adjoint_source = scatter_about(own_keys[0], (VARS, NODES, NODES, NODES, NX, NY, NZ), 1.0, 6.0, ((4, 4), (5, 2), (6, 2)), jnp.float32)
    diagonal = jnp.clip(2.0 + 2.0 * jax.random.uniform(own_keys[1], (VARS, NODES, NODES, NODES, NX, NY, NZ), jnp.float32) ** level_of(own_keys[1], (VARS, NODES, NODES, NODES, NX, NY, NZ), ((4, 4), (5, 2), (6, 2)), -0.2, 0.2), 2.0, 4.0).astype(jnp.bfloat16)
    volume_coupling = scatter_about(own_keys[2], (3, VARS, VARS, NODES, NODES, NODES, NX, NY, NZ), 0.08, 0.5, ((6, 4), (7, 2), (8, 2)))
    surface_coupling = scatter_about(own_keys[3], (6, VARS, VARS, NODES, NODES, NX, NY, NZ), 0.2, 1.1953125, ((5, 4), (6, 2), (7, 2)))
    mortar_owner = draw_mortar_owner(jax.random.fold_in(jax.random.fold_in(keys[10], part), 71), part)
    mortar_fine = draw_mortar_fine(jax.random.fold_in(jax.random.fold_in(keys[10], part), 71), part)
    mortar_coarse = draw_mortar_coarse(jax.random.fold_in(jax.random.fold_in(keys[10], part), 71), part)
    mortar_quarter = set_ends(jax.random.randint(own_keys[7], (HANG,), 0, 4), jax.random.fold_in(own_keys[7], 1), 0, 3).astype(jnp.int32)
    mortar_side = draw_mortar_side(jax.random.fold_in(jax.random.fold_in(keys[10], part), 71), part)
    mortar_coupling = scatter_about(own_keys[9], (HANG, 2, VARS, VARS), 0.4, 2.4, ((0, 16),), jnp.float32)
    return dict(adjoint_source=adjoint_source, diagonal=diagonal, volume_coupling=volume_coupling, surface_coupling=surface_coupling, mortar_owner=mortar_owner, mortar_fine=mortar_fine, mortar_coarse=mortar_coarse, mortar_quarter=mortar_quarter, mortar_side=mortar_side, mortar_coupling=mortar_coupling)


HIGH = lax.Precision.HIGHEST

def node_tables():
    points = np.array([-1.0, -1.0 / np.sqrt(5.0), 1.0 / np.sqrt(5.0), 1.0])
    barycentric = np.array([1.0 / np.prod([points[m] - points[k] for k in range(4) if k != m]) for m in range(4)])
    derivative = np.zeros((4, 4))
    for i in range(4):
        for m in range(4):
            if i != m:
                derivative[i, m] = barycentric[m] / barycentric[i] / (points[i] - points[m])
    for i in range(4):
        derivative[i, i] = -np.sum(derivative[i])
    halves = []
    for h in range(2):
        shifted = (points + 2 * h - 1) / 2.0
        lagrange = np.ones((4, 4))
        for m in range(4):
            for k in range(4):
                if k != m:
                    lagrange[:, m] = lagrange[:, m] * (shifted - points[k]) / (points[m] - points[k])
        halves.append(lagrange)
    projection = np.stack([np.kron(halves[a], halves[b]) for a in range(2) for b in range(2)])
    return (jnp.asarray(derivative, jnp.float32), jnp.asarray(projection, jnp.float32))

def face_trace(values, direction, high_side):
    return lax.index_in_dim(values, 3 * high_side, 1 + direction, keepdims=False)

def trace_rows(values):
    elements = values.shape[4] * values.shape[5] * values.shape[6]
    return jnp.stack([face_trace(values, f // 2, f % 2).reshape(80, elements).T for f in range(6)])

def add_surface(result, surface, direction, high_side):
    position = [slice(None)] * 7
    position[1 + direction] = 3 * high_side
    return result.at[tuple(position)].add(surface)

def add_rows(result, accumulated):
    for f in range(6):
        surface = accumulated[f].T.reshape((5, 4, 4) + result.shape[4:])
        result = add_surface(result, surface, f // 2, f % 2)
    return result

def volume_term(values, volume_coupling, derivative):
    patterns = ['mi,vmjk...->vijk...', 'mj,vimk...->vijk...', 'mk,vijm...->vijk...']
    result = jnp.zeros(values.shape, jnp.float32)
    for direction in range(3):
        slopes = jnp.einsum(patterns[direction], derivative, values, precision=HIGH)
        result = result + jnp.einsum('ab...,b...->a...', volume_coupling[direction].astype(jnp.float32), slopes, precision=HIGH)
    return result

def from_padded(padded, extent):
    neighbour = []
    for f in range(6):
        direction, high_side = (f // 2, f % 2)
        starts = [0, 0, 0, 0, 1, 1, 1]
        starts[4 + direction] = 2 * high_side
        limits = [padded.shape[k] if k < 4 else starts[k] + extent[k - 4] for k in range(7)]
        shifted = lax.slice(padded, starts, limits)
        neighbour.append(face_trace(shifted, direction, 1 - high_side))
    return neighbour

def conforming(result, surface_coupling, neighbour):
    for f in range(6):
        contribution = jnp.einsum('ab...,b...->a...', surface_coupling[f].astype(jnp.float32), neighbour[f], precision=HIGH)
        result = add_surface(result, contribution, f // 2, f % 2)
    return result

def least_squares(hessenberg, initial_norm):
    normal = jnp.dot(hessenberg.T.astype(jnp.float32), hessenberg.astype(jnp.float32), precision=HIGH, preferred_element_type=jnp.float32)
    right_side = initial_norm * hessenberg[0]
    factor = jnp.linalg.cholesky(normal)
    return jax.scipy.linalg.cho_solve((factor, True), right_side)

def reference(adjoint_source, diagonal, volume_coupling, surface_coupling, mortar_owner, mortar_fine, mortar_coarse, mortar_quarter, mortar_side, mortar_coupling):
    derivative, projection = node_tables()
    extent = (NX, NY, NZ)
    hang_rows = jnp.arange(HANG, dtype=jnp.int32)
    device = hang_rows // M_DEV
    dev_x = device // (N_GY * N_GZ)
    dev_y = device // N_GZ % N_GY
    dev_z = device % N_GZ

    def global_number(block_x, local):
        loc_x = local // (CY * CZ)
        loc_y = local // CZ % CY
        loc_z = local % CZ
        return ((block_x * CX + loc_x) * NY + dev_y * CY + loc_y) * NZ + dev_z * CZ + loc_z
    fine_global = global_number(dev_x, mortar_fine).astype(jnp.int32)
    coarse_global = global_number(mortar_owner[:, 0], mortar_coarse).astype(jnp.int32)
    opposite = mortar_side + 1 - 2 * (mortar_side % 2)
    quarter_maps = projection[mortar_quarter]
    diagonal_term = diagonal.astype(jnp.float32)

    def apply(values):
        result = diagonal_term * values + volume_term(values, volume_coupling, derivative)
        padded = jnp.pad(values, [(0, 0)] * 4 + [(1, 1)] * 3)
        result = conforming(result, surface_coupling, from_padded(padded, extent))
        traces = trace_rows(values)
        fine_trace = traces[mortar_side, fine_global].reshape(HANG, 5, 16)
        outbound = jnp.einsum('hab,hbm->ham', mortar_coupling[:, 1], fine_trace, precision=HIGH)
        to_coarse = jnp.einsum('hmc,ham->hac', quarter_maps, outbound, precision=HIGH)
        coarse_trace = traces[opposite, coarse_global].reshape(HANG, 5, 16)
        on_fine = jnp.einsum('hmc,hac->ham', quarter_maps, coarse_trace, precision=HIGH)
        to_fine = jnp.einsum('hab,hbm->ham', mortar_coupling[:, 0], on_fine, precision=HIGH)
        accumulated = jnp.zeros(traces.shape, jnp.float32)
        accumulated = accumulated.at[opposite, coarse_global].add(to_coarse.reshape(HANG, 80))
        accumulated = accumulated.at[mortar_side, fine_global].add(to_fine.reshape(HANG, 80))
        return add_rows(result, accumulated)
    initial_norm = jnp.sqrt(jnp.sum(adjoint_source * adjoint_source) + 1e-06)
    krylov_basis = [adjoint_source / initial_norm]
    hessenberg = jnp.zeros((KRYLOV + 1, KRYLOV), jnp.float32)
    for column in range(KRYLOV):
        mapped = apply(krylov_basis[column])
        for earlier in range(column + 1):
            product = jnp.sum(mapped * krylov_basis[earlier])
            hessenberg = hessenberg.at[earlier, column].set(product)
            mapped = mapped - product * krylov_basis[earlier]
        length = jnp.sqrt(jnp.sum(mapped * mapped) + 1e-06)
        hessenberg = hessenberg.at[column + 1, column].set(length)
        if column + 1 < KRYLOV:
            krylov_basis.append(mapped / length)
    weights = least_squares(hessenberg, initial_norm)
    solution = jnp.zeros(adjoint_source.shape, jnp.float32)
    for column in range(KRYLOV):
        solution = solution + weights[column] * krylov_basis[column]
    return solution
```

```python
import functools

import jax
import jax.numpy as jnp
import ml_dtypes
import numpy as np
from jax import lax
from jax.experimental import pallas as pl
from jax.experimental.pallas import tpu as pltpu
from jax.sharding import PartitionSpec as P

KRYLOV = 4
SHIFT = 3.0
F32 = jnp.float32
BF16 = jnp.bfloat16
LANES = 128
MESH = pl.DeviceIdType.MESH


def node_tables():
    points = np.array([-1.0, -1.0 / np.sqrt(5.0), 1.0 / np.sqrt(5.0), 1.0])
    barycentric = np.array(
        [1.0 / np.prod([points[m] - points[k] for k in range(4) if k != m]) for m in range(4)]
    )
    derivative = np.zeros((4, 4))
    for i in range(4):
        for m in range(4):
            if i != m:
                derivative[i, m] = barycentric[m] / barycentric[i] / (points[i] - points[m])
    for i in range(4):
        derivative[i, i] = -np.sum(derivative[i])
    halves = []
    for h in range(2):
        shifted = (points + 2 * h - 1) / 2.0
        lagrange = np.ones((4, 4))
        for m in range(4):
            for k in range(4):
                if k != m:
                    lagrange[:, m] = (
                        lagrange[:, m] * (shifted - points[k]) / (points[m] - points[k])
                    )
        halves.append(lagrange)
    return derivative.astype(np.float32), np.stack(halves).astype(np.float32)


def split(value):
    high = value.astype(BF16)
    return high, (value - high.astype(F32)).astype(BF16)


def node_matrices():
    derivative, _ = node_tables()
    eye = np.eye(4, dtype=np.float32)
    slopes = [
        np.kron(np.kron(derivative.T, eye), eye),
        np.kron(np.kron(eye, derivative.T), eye),
        np.kron(np.kron(eye, eye), derivative.T),
    ]
    traces = []
    for node in (0, 3):
        traces.append(np.kron(np.kron(eye, eye[node : node + 1]), eye))
    for node in (0, 3):
        traces.append(np.kron(np.kron(eye, eye), eye[node : node + 1]))
    traces = np.concatenate(traces)
    rows = np.concatenate(slopes + [traces])
    high = rows.astype(ml_dtypes.bfloat16)
    low = (rows - high.astype(np.float32)).astype(ml_dtypes.bfloat16)
    forward = np.concatenate([high, high, low, low], axis=1)
    back = np.concatenate([traces.T, traces.T], axis=1).astype(ml_dtypes.bfloat16)
    return forward, back


def small_solve(gram):
    size = KRYLOV + 1
    norm = jnp.sqrt(gram[0][0] + 1e-6)
    one = jnp.ones_like(norm)
    basis = [[one / norm]]
    images = [[gram[0][i] / norm for i in range(size)]]
    hess = [[None] * KRYLOV for _ in range(size)]
    for column in range(KRYLOV):
        current = basis[column]
        mapped = [SHIFT * c for c in current] + [None]
        for i, c in enumerate(current):
            mapped[i + 1] = c if mapped[i + 1] is None else mapped[i + 1] + c
        for earlier in range(column + 1):
            product = sum(m * images[earlier][i] for i, m in enumerate(mapped))
            hess[earlier][column] = product
            for i, c in enumerate(basis[earlier]):
                mapped[i] = mapped[i] - product * c
        image = [sum(m * gram[k][i] for k, m in enumerate(mapped)) for i in range(size)]
        square = sum(m * image[i] for i, m in enumerate(mapped))
        length = jnp.sqrt(jnp.maximum(square, 0.0) + 1e-6)
        hess[column + 1][column] = length
        if column + 1 < KRYLOV:
            scale = one / length
            basis.append([m * scale for m in mapped])
            images.append([m * scale for m in image])
    normal = [[None] * KRYLOV for _ in range(KRYLOV)]
    for i in range(KRYLOV):
        for j in range(i + 1):
            normal[i][j] = sum(hess[r][i] * hess[r][j] for r in range(j + 2))
    factor = [[None] * KRYLOV for _ in range(KRYLOV)]
    inverse = [None] * KRYLOV
    for j in range(KRYLOV):
        pivot = normal[j][j]
        for k in range(j):
            pivot = pivot - factor[j][k] * factor[j][k]
        factor[j][j] = jnp.sqrt(pivot)
        inverse[j] = one / factor[j][j]
        for i in range(j + 1, KRYLOV):
            value = normal[i][j]
            for k in range(j):
                value = value - factor[i][k] * factor[j][k]
            factor[i][j] = value * inverse[j]
    half = []
    for i in range(KRYLOV):
        value = norm * hess[0][i]
        for k in range(i):
            value = value - factor[i][k] * half[k]
        half.append(value * inverse[i])
    weights = [None] * KRYLOV
    for i in reversed(range(KRYLOV)):
        value = half[i]
        for k in range(i + 1, KRYLOV):
            value = value - factor[k][i] * weights[k]
        weights[i] = value * inverse[i]
    return [
        sum(weights[j] * basis[j][i] for j in range(i, KRYLOV)) for i in range(KRYLOV)
    ]


def kernel(
    sizes,
    source,
    diagonal,
    volume,
    surface,
    pack,
    forward,
    back,
    out,
    xs,
    slopes,
    right,
    traces,
    halo_x,
    halo_y,
    halo_z,
    neighbour_pack,
    gather_left,
    pick_own,
    pick_halo,
    place,
    coupling,
    maps,
    rows,
    rows_left,
    faces,
    faces_left,
    gram,
    message,
    messages,
    send_sem,
    recv_sem,
    pack_send,
    pack_recv,
    sum_send,
    sum_recv,
):
    axes = ("gx", "gy", "gz")
    here = [lax.axis_index(a) for a in axes]
    group = sizes[0] * sizes[1] * sizes[2]
    me = (here[0] * sizes[1] + here[1]) * sizes[2] + here[2]
    has_low = [h > 0 for h in here]
    has_high = [h < n - 1 for h, n in zip(here, sizes)]

    def peer(step):
        other = lax.rem(me + step, group)
        return {
            "gx": other // (sizes[1] * sizes[2]),
            "gy": lax.rem(other // sizes[2], sizes[1]),
            "gz": lax.rem(other, sizes[2]),
        }

    barrier = pltpu.get_barrier_semaphore()

    @pl.loop(1, group)
    def _(step):
        pl.semaphore_signal(barrier, inc=1, device_id=peer(step), device_id_type=MESH)

    xs[0] = source[...]
    halos = (halo_x, halo_y, halo_z)
    for d in range(3):
        for s, there in ((0, has_low[d]), (1, has_high[d])):

            @pl.when(jnp.logical_not(there))
            def _(d=d, s=s):
                for k in range(KRYLOV):
                    halos[d][k, s] = jnp.zeros((5, 16, LANES), F32)

                if d == 0:
                    neighbour_pack[s] = jnp.full((32, LANES), -9.0, F32)

    pl.semaphore_wait(barrier, group - 1)

    def to(d, s):
        return {axes[d]: here[d] - 1 if s == 0 else here[d] + 1}

    def pack_copy(s):
        return pltpu.make_async_remote_copy(
            src_ref=pack,
            dst_ref=neighbour_pack.at[1 - s],
            send_sem=pack_send.at[s],
            recv_sem=pack_recv.at[s],
            device_id=to(0, s),
            device_id_type=MESH,
        )

    def face_copy(d, s, k):
        if d == 0:
            face = xs.at[k, :, pl.ds(48 * s, 16), :]
        else:
            face = traces.at[k, 2 * (d - 1) + s]
        return pltpu.make_async_remote_copy(
            src_ref=face,
            dst_ref=halos[d].at[k, 1 - s],
            send_sem=send_sem.at[k, d, s],
            recv_sem=recv_sem.at[k, d, s],
            device_id=to(d, s),
            device_id_type=MESH,
        )

    def sides(d, s):
        return (has_low[d], has_high[d]) if s == 0 else (has_high[d], has_low[d])

    def start(d, k):
        for s in range(2):
            target, _ = sides(d, s)

            @pl.when(target)
            def _(s=s):
                face_copy(d, s, k).start()

    def arrive(d, k):
        for s in range(2):
            target, origin = sides(d, s)

            @pl.when(origin)
            def _(s=s):
                face_copy(d, s, k).wait_recv()

            @pl.when(target)
            def _(s=s):
                face_copy(d, s, k).wait_send()

    for s in range(2):

        @pl.when(sides(0, s)[0])
        def _(s=s):
            pack_copy(s).start()

    lane = lax.broadcasted_iota(jnp.int32, (1, LANES), 1)
    left_half = lane < 64
    _, halves = node_tables()

    def keys(packed, me_x):
        offset = packed[25:26] - me_x
        fine, coarse, quarter, side = (packed[r : r + 1] for r in range(26, 30))
        odd = jnp.floor(side * 0.5)
        opposite = side + 1.0 - 2.0 * (side - 2.0 * odd)
        return offset, fine, coarse, quarter, side, opposite

    def one_hot(key, count):
        index = lax.broadcasted_iota(jnp.int32, (count, LANES), 0).astype(F32)
        return jnp.where(index == key, 1.0, 0.0).astype(BF16)

    def make_maps(slot, quarter, flipped):
        first = quarter >= 2.0
        second = (quarter - 2.0 * jnp.where(first, 1.0, 0.0)) >= 1.0
        for stage, bit in ((0, first), (1, second)):
            for i in range(4):
                for m in range(4):
                    straight = jnp.where(bit, float(halves[1, i, m]), float(halves[0, i, m]))
                    turned = jnp.where(bit, float(halves[1, m, i]), float(halves[0, m, i]))
                    row = 16 * stage + 4 * i + m
                    maps[slot, row : row + 1] = jnp.where(flipped, turned, straight)

    own = pack[...]
    place_x = here[0].astype(F32)
    offset, fine, coarse, quarter, side, opposite = keys(own, place_x)
    same = offset == 0.0
    at_coarse = jnp.where(same, opposite * LANES + coarse, -1.0)
    at_fine = side * LANES + fine
    pick_own[...] = one_hot(
        jnp.where(left_half, at_coarse, jnp.where(same, at_fine, -1.0)), 768
    )
    outside = jnp.where(offset < 0.0, coarse, LANES + coarse)
    pick_halo[:, 0:128] = one_hot(
        jnp.where(left_half & jnp.logical_not(same), outside, -1.0), 256
    )
    place[:, 0:128] = one_hot(jnp.where(left_half, at_fine, at_coarse), 768)
    coupling[0] = own
    make_maps(0, quarter, jnp.logical_not(left_half))

    def from_neighbours():
        for s in range(2):
            target, origin = sides(0, s)

            @pl.when(origin)
            def _(s=s):
                pack_copy(s).wait_recv()

            @pl.when(target)
            def _(s=s):
                pack_copy(s).wait_send()

        both = jnp.where(left_half, pltpu.roll(neighbour_pack[0], 64, 1), neighbour_pack[1])
        offset, fine, coarse, quarter, _, _ = keys(both, place_x)
        valid = offset == 0.0
        base = jnp.where(left_half, 0.0, 1.0 * LANES)
        pick_halo[:, 128:256] = one_hot(jnp.where(valid, base + fine, -1.0), 256)
        place[:, 128:256] = one_hot(jnp.where(valid, base + coarse, -1.0), 768)
        coupling[1] = jnp.where(valid, both, 0.0)
        make_maps(1, jnp.where(valid, quarter, 0.0), lane >= 0)

    def put_trace(block, var, value):
        high, low = split(value)
        columns = pl.ds(block * LANES, LANES)
        gather_left[pl.ds(16 * var, 16), columns] = high
        gather_left[pl.ds(80 + 16 * var, 16), columns] = low

    def products(k, count):
        @pl.loop(0, count)
        def _(i):
            total = jnp.zeros((8, LANES), F32)
            for b in range(5):
                both = xs[k, b] * xs[i, b]
                for r in range(8):
                    total = total + both[8 * r : 8 * r + 8]
            gram[pl.ds(k * 8 + i, 1), :] = jnp.sum(total, axis=0, keepdims=True)

    gram[...] = jnp.zeros_like(gram)

    @pl.loop(0, KRYLOV)
    def _(k):
        start(0, k)
        for b in range(5):
            high, low = split(xs[k, b])
            columns = slice(b * LANES, (b + 1) * LANES)
            right[0:64, columns] = high
            right[64:128, columns] = low
            right[128:192, columns] = high
            right[192:256, columns] = low
        slopes[...] = jnp.dot(forward[...], right[...], preferred_element_type=F32)
        for f in range(4):
            for b in range(5):
                traces[k, f, b] = slopes[
                    192 + 16 * f : 208 + 16 * f, b * LANES : (b + 1) * LANES
                ]
        start(1, k)
        start(2, k)

        @pl.when(k == 0)
        def _():
            from_neighbours()

        for b in range(5):
            put_trace(0, b, xs[k, b, 0:16])
            put_trace(1, b, xs[k, b, 48:64])
            for f in range(4):
                put_trace(2 + f, b, traces[k, f, b])
        gathered = jnp.dot(
            gather_left[:, 0:768], pick_own[...], preferred_element_type=F32
        )
        rows[0] = gathered[0:80] + gathered[80:160]

        @pl.loop(0, 4)
        def _(c):
            chunk = pl.ds(pl.multiple_of(16 * c, 16), 16)
            total = [
                (diagonal[a, chunk].astype(F32) - SHIFT) * xs[k, a, chunk] for a in range(5)
            ]
            for d in range(3):
                for b in range(5):
                    slope = slopes[
                        pl.ds(pl.multiple_of(64 * d + 16 * c, 16), 16),
                        b * LANES : (b + 1) * LANES,
                    ]
                    for a in range(5):
                        total[a] = total[a] + volume[d, a, b, chunk].astype(F32) * slope
            for a in range(5):
                xs[k + 1, a, chunk] = total[a]

        products(k, k + 1)
        arrive(0, k)
        arrive(1, k)
        arrive(2, k)
        for s in range(2):
            for b in range(5):
                put_trace(6 + s, b, halo_x[k, s, b])
        gathered = jnp.dot(
            gather_left[:, 768:1024], pick_halo[...], preferred_element_type=F32
        )
        gathered = gathered[0:80] + gathered[80:160]
        rows[0] = rows[0] + gathered[:, 0:128]
        rows[1] = gathered[:, 128:256]
        for g in range(2):
            before = [rows[g, 16 * b : 16 * b + 16] for b in range(5)]
            for a in range(5):
                value = coupling[g, 5 * a : 5 * a + 1] * before[0]
                for b in range(1, 5):
                    row = 5 * a + b
                    value = value + coupling[g, row : row + 1] * before[b]
                rows[g, 16 * a : 16 * a + 16] = value
            nodes = [rows[g, pl.ds(m, 5, stride=16), :] for m in range(16)]
            for stage in range(2):
                after = [None] * 16
                for i in range(4):
                    for j in range(4):
                        own_index = i if stage == 0 else j
                        for m in range(4):
                            row = 16 * stage + 4 * own_index + m
                            node = 4 * m + j if stage == 0 else 4 * i + m
                            term = maps[g, row : row + 1] * nodes[node]
                            at = 4 * i + j
                            after[at] = term if m == 0 else after[at] + term
                nodes = after
            for m in range(16):
                rows[g, pl.ds(m, 5, stride=16), :] = nodes[m]
            high, low = split(rows[g])
            rows_left[0:80, g * LANES : (g + 1) * LANES] = high
            rows_left[80:160, g * LANES : (g + 1) * LANES] = low
        faces[...] = lax.dot_general(
            rows_left[...], place[...], (((1,), (1,)), ((), ())), preferred_element_type=F32
        )
        for f in range(6):
            d, s = f // 2, f % 2
            if d == 0:
                beside = [halo_x[k, s, b] for b in range(5)]
            elif d == 1:
                beside = [halo_y[k, s, b] for b in range(5)]
            else:
                edge = lane == (LANES - 1 if s == 0 else 0)
                turn = 1 if s == 0 else LANES - 1
                beside = [
                    pltpu.roll(
                        jnp.where(edge, halo_z[k, s, b], traces[k, 3 - s, b]), turn, 1
                    )
                    for b in range(5)
                ]
            columns = slice(f * LANES, (f + 1) * LANES)
            for a in range(5):
                value = (
                    faces[16 * a : 16 * a + 16, columns]
                    + faces[80 + 16 * a : 96 + 16 * a, columns]
                )
                for b in range(5):
                    value = value + surface[f, a, b].astype(F32) * beside[b]
                if d == 0:
                    at = 48 * s
                    xs[k + 1, a, at : at + 16] = xs[k + 1, a, at : at + 16] + value
                else:
                    high, low = split(value)
                    at = 16 * (f - 2)
                    faces_left[at : at + 16, a * LANES : (a + 1) * LANES] = high
                    faces_left[64 + at : 80 + at, a * LANES : (a + 1) * LANES] = low
        added = jnp.dot(back[...], faces_left[...], preferred_element_type=F32)
        for a in range(5):
            xs[k + 1, a] = xs[k + 1, a] + added[:, a * LANES : (a + 1) * LANES]

    products(KRYLOV, KRYLOV + 1)
    message[...] = lax.dot_general(
        jnp.ones((8, LANES), F32),
        gram[...],
        (((1,), (1,)), ((), ())),
        preferred_element_type=F32,
        precision=lax.Precision.HIGHEST,
    )

    def sum_copy(step):
        return pltpu.make_async_remote_copy(
            src_ref=message,
            dst_ref=messages.at[step],
            send_sem=sum_send.at[step],
            recv_sem=sum_recv.at[step],
            device_id=peer(step),
            device_id_type=MESH,
        )

    @pl.loop(1, group)
    def _(step):
        sum_copy(step).start()

    messages[0] = message[...]

    @pl.loop(1, group)
    def _(step):
        sum_copy(step).wait_recv()

    @pl.loop(1, group)
    def _(step):
        sum_copy(step).wait_send()

    def add(i, total):
        return total + messages[lax.rem(i + group - me, group)]

    total = lax.fori_loop(0, group, add, jnp.zeros((8, LANES), F32))
    size = KRYLOV + 1
    entries = [[None] * size for _ in range(size)]
    for k in range(size):
        for i in range(k + 1):
            entry = jnp.sum(jnp.where(lane == 8 * k + i, total, 0.0), axis=1, keepdims=True)
            entry = jnp.broadcast_to(entry, (8, LANES))
            entries[k][i] = entries[i][k] = entry
    scales = small_solve(entries)
    for b in range(5):
        for r in range(8):
            at = slice(8 * r, 8 * r + 8)
            value = scales[0] * xs[0, b, at]
            for k in range(1, KRYLOV):
                value = value + scales[k] * xs[k, b, at]
            out[b, at] = value


def local(
    sizes,
    adjoint_source,
    diagonal,
    volume_coupling,
    surface_coupling,
    mortar_owner,
    mortar_fine,
    mortar_coarse,
    mortar_quarter,
    mortar_side,
    mortar_coupling,
):
    forward, back = node_matrices()
    count = mortar_fine.shape[0]
    numbers = jnp.stack(
        [mortar_owner[:, 0], mortar_fine, mortar_coarse, mortar_quarter, mortar_side]
    ).astype(F32)
    pairs = mortar_coupling.reshape(count, 2, 25).transpose(2, 1, 0).reshape(25, 2 * count)
    pack = jnp.concatenate(
        [pairs, jnp.concatenate([numbers, numbers], axis=1), jnp.zeros((2, 2 * count), F32)]
    )
    group = sizes[0] * sizes[1] * sizes[2]
    vmem = pl.BlockSpec(memory_space=pltpu.VMEM)
    dma = pltpu.SemaphoreType.DMA
    result = pl.pallas_call(
        functools.partial(kernel, sizes),
        out_shape=jax.ShapeDtypeStruct((5, 64, LANES), F32),
        in_specs=[vmem] * 7,
        out_specs=vmem,
        scratch_shapes=[
            pltpu.VMEM((KRYLOV + 1, 5, 64, LANES), F32),
            pltpu.VMEM((256, 5 * LANES), F32),
            pltpu.VMEM((256, 5 * LANES), BF16),
            pltpu.VMEM((KRYLOV, 4, 5, 16, LANES), F32),
            pltpu.VMEM((KRYLOV, 2, 5, 16, LANES), F32),
            pltpu.VMEM((KRYLOV, 2, 5, 16, LANES), F32),
            pltpu.VMEM((KRYLOV, 2, 5, 16, LANES), F32),
            pltpu.VMEM((2, 32, LANES), F32),
            pltpu.VMEM((160, 8 * LANES), BF16),
            pltpu.VMEM((6 * LANES, LANES), BF16),
            pltpu.VMEM((2 * LANES, 2 * LANES), BF16),
            pltpu.VMEM((6 * LANES, 2 * LANES), BF16),
            pltpu.VMEM((2, 32, LANES), F32),
            pltpu.VMEM((2, 32, LANES), F32),
            pltpu.VMEM((2, 80, LANES), F32),
            pltpu.VMEM((160, 2 * LANES), BF16),
            pltpu.VMEM((160, 6 * LANES), F32),
            pltpu.VMEM((128, 5 * LANES), BF16),
            pltpu.VMEM((LANES, LANES), F32),
            pltpu.VMEM((8, LANES), F32),
            pltpu.VMEM((group, 8, LANES), F32),
            dma((KRYLOV, 3, 2)),
            dma((KRYLOV, 3, 2)),
            dma((2,)),
            dma((2,)),
            dma((group,)),
            dma((group,)),
        ],
        compiler_params=pltpu.CompilerParams(
            collective_id=0, has_side_effects=True, vmem_limit_bytes=48 * 1024 * 1024
        ),
    )(
        adjoint_source.reshape(5, 64, LANES),
        diagonal.reshape(5, 64, LANES),
        volume_coupling.reshape(3, 5, 5, 64, LANES),
        surface_coupling.reshape(6, 5, 5, 16, LANES),
        pack,
        jnp.asarray(forward),
        jnp.asarray(back),
    )
    return result.reshape(adjoint_source.shape)


def solution(mesh):
    placed = (
        P(None, None, None, None, ("groups", "gx"), "gy", "gz"),
        P(None, None, None, None, ("groups", "gx"), "gy", "gz"),
        P(None, None, None, None, None, None, ("groups", "gx"), "gy", "gz"),
        P(None, None, None, None, None, ("groups", "gx"), "gy", "gz"),
        P(("groups", "gx", "gy", "gz"), None),
        P(("groups", "gx", "gy", "gz")),
        P(("groups", "gx", "gy", "gz")),
        P(("groups", "gx", "gy", "gz")),
        P(("groups", "gx", "gy", "gz")),
        P(("groups", "gx", "gy", "gz"), None, None, None),
    )
    sizes = tuple(mesh.shape[a] for a in ("gx", "gy", "gz"))
    return jax.shard_map(
        functools.partial(local, sizes),
        mesh=mesh,
        in_specs=placed,
        out_specs=P(None, None, None, None, ("groups", "gx"), "gy", "gz"),
        check_vma=False,
    )
```

```python
import functools

import jax
import jax.numpy as jnp
import ml_dtypes
import numpy as np
from jax import lax
from jax.experimental import pallas as pl
from jax.experimental.pallas import tpu as pltpu
from jax.sharding import PartitionSpec as P

KRYLOV = 4
SHIFT = 3.0
F32 = jnp.float32
BF16 = jnp.bfloat16
LANES = 128
MESH = pl.DeviceIdType.MESH


def node_tables():
    points = np.array([-1.0, -1.0 / np.sqrt(5.0), 1.0 / np.sqrt(5.0), 1.0])
    barycentric = np.array(
        [1.0 / np.prod([points[m] - points[k] for k in range(4) if k != m]) for m in range(4)]
    )
    derivative = np.zeros((4, 4))
    for i in range(4):
        for m in range(4):
            if i != m:
                derivative[i, m] = barycentric[m] / barycentric[i] / (points[i] - points[m])
    for i in range(4):
        derivative[i, i] = -np.sum(derivative[i])
    halves = []
    for h in range(2):
        shifted = (points + 2 * h - 1) / 2.0
        lagrange = np.ones((4, 4))
        for m in range(4):
            for k in range(4):
                if k != m:
                    lagrange[:, m] = (
                        lagrange[:, m] * (shifted - points[k]) / (points[m] - points[k])
                    )
        halves.append(lagrange)
    return derivative.astype(np.float32), np.stack(halves).astype(np.float32)


def split(value):
    high = value.astype(BF16)
    return high, (value - high.astype(F32)).astype(BF16)


def node_matrices():
    derivative, _ = node_tables()
    eye = np.eye(4, dtype=np.float32)
    slopes = [
        np.kron(np.kron(derivative.T, eye), eye),
        np.kron(np.kron(eye, derivative.T), eye),
        np.kron(np.kron(eye, eye), derivative.T),
    ]
    traces = []
    for node in (0, 3):
        traces.append(np.kron(np.kron(eye, eye[node : node + 1]), eye))
    for node in (0, 3):
        traces.append(np.kron(np.kron(eye, eye), eye[node : node + 1]))
    traces = np.concatenate(traces)
    rows = np.concatenate(slopes + [traces])
    high = rows.astype(ml_dtypes.bfloat16)
    low = (rows - high.astype(np.float32)).astype(ml_dtypes.bfloat16)
    forward = np.concatenate([high, high, low, low], axis=1)
    back = np.concatenate([traces.T, traces.T], axis=1).astype(ml_dtypes.bfloat16)
    return forward, back


def small_solve(gram):
    size = KRYLOV + 1
    norm = jnp.sqrt(gram[0][0] + 1e-6)
    one = jnp.ones_like(norm)
    basis = [[one / norm]]
    images = [[gram[0][i] / norm for i in range(size)]]
    hess = [[None] * KRYLOV for _ in range(size)]
    for column in range(KRYLOV):
        current = basis[column]
        mapped = [SHIFT * c for c in current] + [None]
        for i, c in enumerate(current):
            mapped[i + 1] = c if mapped[i + 1] is None else mapped[i + 1] + c
        for earlier in range(column + 1):
            product = sum(m * images[earlier][i] for i, m in enumerate(mapped))
            hess[earlier][column] = product
            for i, c in enumerate(basis[earlier]):
                mapped[i] = mapped[i] - product * c
        image = [sum(m * gram[k][i] for k, m in enumerate(mapped)) for i in range(size)]
        square = sum(m * image[i] for i, m in enumerate(mapped))
        length = jnp.sqrt(jnp.maximum(square, 0.0) + 1e-6)
        hess[column + 1][column] = length
        if column + 1 < KRYLOV:
            scale = one / length
            basis.append([m * scale for m in mapped])
            images.append([m * scale for m in image])
    normal = [[None] * KRYLOV for _ in range(KRYLOV)]
    for i in range(KRYLOV):
        for j in range(i + 1):
            normal[i][j] = sum(hess[r][i] * hess[r][j] for r in range(j + 2))
    factor = [[None] * KRYLOV for _ in range(KRYLOV)]
    inverse = [None] * KRYLOV
    for j in range(KRYLOV):
        pivot = normal[j][j]
        for k in range(j):
            pivot = pivot - factor[j][k] * factor[j][k]
        factor[j][j] = jnp.sqrt(pivot)
        inverse[j] = one / factor[j][j]
        for i in range(j + 1, KRYLOV):
            value = normal[i][j]
            for k in range(j):
                value = value - factor[i][k] * factor[j][k]
            factor[i][j] = value * inverse[j]
    half = []
    for i in range(KRYLOV):
        value = norm * hess[0][i]
        for k in range(i):
            value = value - factor[i][k] * half[k]
        half.append(value * inverse[i])
    weights = [None] * KRYLOV
    for i in reversed(range(KRYLOV)):
        value = half[i]
        for k in range(i + 1, KRYLOV):
            value = value - factor[k][i] * weights[k]
        weights[i] = value * inverse[i]
    return [
        sum(weights[j] * basis[j][i] for j in range(i, KRYLOV)) for i in range(KRYLOV)
    ]


def kernel(
    sizes,
    source_hbm,
    diagonal_hbm,
    volume_hbm,
    surface_hbm,
    owner_hbm,
    fine_hbm,
    coarse_hbm,
    quarter_hbm,
    side_hbm,
    coupling_hbm,
    forward_hbm,
    back_hbm,
    out,
    diagonal,
    volume,
    surface,
    numbers,
    pairs,
    forward,
    back,
    pack,
    load_sem,
    xs,
    slopes,
    right,
    traces,
    halo_x,
    halo_y,
    halo_z,
    neighbour_pack,
    gather_left,
    pick_own,
    pick_halo,
    place,
    coupling,
    maps,
    rows,
    rows_left,
    faces,
    faces_left,
    gram,
    message,
    messages,
    send_sem,
    recv_sem,
    pack_send,
    pack_recv,
    sum_send,
    sum_recv,
):
    axes = ("gx", "gy", "gz")
    here = [lax.axis_index(a) for a in axes]
    group = sizes[0] * sizes[1] * sizes[2]
    me = (here[0] * sizes[1] + here[1]) * sizes[2] + here[2]
    has_low = [h > 0 for h in here]
    has_high = [h < n - 1 for h, n in zip(here, sizes)]

    def peer(step):
        other = lax.rem(me + step, group)
        return {
            "gx": other // (sizes[1] * sizes[2]),
            "gy": lax.rem(other // sizes[2], sizes[1]),
            "gz": lax.rem(other, sizes[2]),
        }

    loads = [
        pltpu.make_async_copy(origin, target, load_sem.at[i])
        for i, (origin, target) in enumerate(
            (
                (source_hbm, xs.at[0]),
                (owner_hbm, numbers.at[0]),
                (fine_hbm, numbers.at[1]),
                (coarse_hbm, numbers.at[2]),
                (quarter_hbm, numbers.at[3]),
                (side_hbm, numbers.at[4]),
                (coupling_hbm, pairs),
                (forward_hbm, forward),
                (diagonal_hbm, diagonal),
                (volume_hbm, volume),
                (surface_hbm, surface),
                (back_hbm, back),
            )
        )
    ]
    for load in loads:
        load.start()
    barrier = pltpu.get_barrier_semaphore()

    @pl.loop(1, group)
    def _(step):
        pl.semaphore_signal(barrier, inc=1, device_id=peer(step), device_id_type=MESH)

    halos = (halo_x, halo_y, halo_z)
    for d in range(3):
        for s, there in ((0, has_low[d]), (1, has_high[d])):

            @pl.when(jnp.logical_not(there))
            def _(d=d, s=s):
                for k in range(KRYLOV):
                    halos[d][k, s] = jnp.zeros((5, 16, LANES), F32)

                if d == 0:
                    neighbour_pack[s] = jnp.full((32, LANES), -9.0, F32)

    for load in loads[1:7]:
        load.wait()
    for half in range(2):
        at = slice(64 * half, 64 * half + 64)
        pack[0:25, at] = pairs[:, half, :]
        for i in range(5):
            pack[25 + i : 26 + i, at] = numbers[i].astype(F32)
    pack[30:32] = jnp.zeros((2, LANES), F32)
    pl.semaphore_wait(barrier, group - 1)

    def to(d, s):
        return {axes[d]: here[d] - 1 if s == 0 else here[d] + 1}

    def pack_copy(s):
        return pltpu.make_async_remote_copy(
            src_ref=pack,
            dst_ref=neighbour_pack.at[1 - s],
            send_sem=pack_send.at[s],
            recv_sem=pack_recv.at[s],
            device_id=to(0, s),
            device_id_type=MESH,
        )

    def face_copy(d, s, k):
        if d == 0:
            face = xs.at[k, :, pl.ds(48 * s, 16), :]
        else:
            face = traces.at[k, 2 * (d - 1) + s]
        return pltpu.make_async_remote_copy(
            src_ref=face,
            dst_ref=halos[d].at[k, 1 - s],
            send_sem=send_sem.at[k, d, s],
            recv_sem=recv_sem.at[k, d, s],
            device_id=to(d, s),
            device_id_type=MESH,
        )

    def sides(d, s):
        return (has_low[d], has_high[d]) if s == 0 else (has_high[d], has_low[d])

    def start(d, k):
        for s in range(2):
            target, _ = sides(d, s)

            @pl.when(target)
            def _(s=s):
                face_copy(d, s, k).start()

    def arrive(d, k):
        for s in range(2):
            target, origin = sides(d, s)

            @pl.when(origin)
            def _(s=s):
                face_copy(d, s, k).wait_recv()

            @pl.when(target)
            def _(s=s):
                face_copy(d, s, k).wait_send()

    for s in range(2):

        @pl.when(sides(0, s)[0])
        def _(s=s):
            pack_copy(s).start()

    lane = lax.broadcasted_iota(jnp.int32, (1, LANES), 1)
    left_half = lane < 64
    _, halves = node_tables()

    def keys(packed, me_x):
        offset = packed[25:26] - me_x
        fine, coarse, quarter, side = (packed[r : r + 1] for r in range(26, 30))
        odd = jnp.floor(side * 0.5)
        opposite = side + 1.0 - 2.0 * (side - 2.0 * odd)
        return offset, fine, coarse, quarter, side, opposite

    def one_hot(key, count):
        index = lax.broadcasted_iota(jnp.int32, (count, LANES), 0).astype(F32)
        return jnp.where(index == key, 1.0, 0.0).astype(BF16)

    def make_maps(slot, quarter, flipped):
        first = quarter >= 2.0
        second = (quarter - 2.0 * jnp.where(first, 1.0, 0.0)) >= 1.0
        for stage, bit in ((0, first), (1, second)):
            for i in range(4):
                for m in range(4):
                    straight = jnp.where(bit, float(halves[1, i, m]), float(halves[0, i, m]))
                    turned = jnp.where(bit, float(halves[1, m, i]), float(halves[0, m, i]))
                    row = 16 * stage + 4 * i + m
                    maps[slot, row : row + 1] = jnp.where(flipped, turned, straight)

    place_x = here[0].astype(F32)

    def from_own():
        own = pack[...]
        offset, fine, coarse, quarter, side, opposite = keys(own, place_x)
        same = offset == 0.0
        at_coarse = jnp.where(same, opposite * LANES + coarse, -1.0)
        at_fine = side * LANES + fine
        pick_own[...] = one_hot(
            jnp.where(left_half, at_coarse, jnp.where(same, at_fine, -1.0)), 768
        )
        outside = jnp.where(offset < 0.0, coarse, LANES + coarse)
        pick_halo[:, 0:128] = one_hot(
            jnp.where(left_half & jnp.logical_not(same), outside, -1.0), 256
        )
        place[:, 0:128] = one_hot(jnp.where(left_half, at_fine, at_coarse), 768)
        coupling[0] = own
        make_maps(0, quarter, jnp.logical_not(left_half))

    def from_neighbours():
        for s in range(2):
            target, origin = sides(0, s)

            @pl.when(origin)
            def _(s=s):
                pack_copy(s).wait_recv()

            @pl.when(target)
            def _(s=s):
                pack_copy(s).wait_send()

        both = jnp.where(left_half, pltpu.roll(neighbour_pack[0], 64, 1), neighbour_pack[1])
        offset, fine, coarse, quarter, _, _ = keys(both, place_x)
        valid = offset == 0.0
        base = jnp.where(left_half, 0.0, 1.0 * LANES)
        pick_halo[:, 128:256] = one_hot(jnp.where(valid, base + fine, -1.0), 256)
        place[:, 128:256] = one_hot(jnp.where(valid, base + coarse, -1.0), 768)
        coupling[1] = jnp.where(valid, both, 0.0)
        make_maps(1, jnp.where(valid, quarter, 0.0), lane >= 0)

    def put_trace(block, var, value):
        high, low = split(value)
        columns = pl.ds(block * LANES, LANES)
        gather_left[pl.ds(16 * var, 16), columns] = high
        gather_left[pl.ds(80 + 16 * var, 16), columns] = low

    def products(k, count):
        @pl.loop(0, count)
        def _(i):
            total = jnp.zeros((8, LANES), F32)
            for b in range(5):
                both = xs[k, b] * xs[i, b]
                for r in range(8):
                    total = total + both[8 * r : 8 * r + 8]
            gram[pl.ds(k * 8 + i, 1), :] = jnp.sum(total, axis=0, keepdims=True)

    gram[...] = jnp.zeros_like(gram)
    loads[0].wait()

    @pl.loop(0, KRYLOV)
    def _(k):
        start(0, k)
        for b in range(5):
            high, low = split(xs[k, b])
            columns = slice(b * LANES, (b + 1) * LANES)
            right[0:64, columns] = high
            right[64:128, columns] = low
            right[128:192, columns] = high
            right[192:256, columns] = low

        @pl.when(k == 0)
        def _():
            loads[7].wait()

        slopes[...] = jnp.dot(forward[...], right[...], preferred_element_type=F32)
        for f in range(4):
            for b in range(5):
                traces[k, f, b] = slopes[
                    192 + 16 * f : 208 + 16 * f, b * LANES : (b + 1) * LANES
                ]
        start(1, k)
        start(2, k)

        @pl.when(k == 0)
        def _():
            from_own()
            loads[8].wait()
            loads[9].wait()

        for b in range(5):
            put_trace(0, b, xs[k, b, 0:16])
            put_trace(1, b, xs[k, b, 48:64])
            for f in range(4):
                put_trace(2 + f, b, traces[k, f, b])
        gathered = jnp.dot(
            gather_left[:, 0:768], pick_own[...], preferred_element_type=F32
        )
        rows[0] = gathered[0:80] + gathered[80:160]

        @pl.loop(0, 4)
        def _(c):
            chunk = pl.ds(pl.multiple_of(16 * c, 16), 16)
            total = [
                (diagonal[a, chunk].astype(F32) - SHIFT) * xs[k, a, chunk] for a in range(5)
            ]
            for d in range(3):
                for b in range(5):
                    slope = slopes[
                        pl.ds(pl.multiple_of(64 * d + 16 * c, 16), 16),
                        b * LANES : (b + 1) * LANES,
                    ]
                    for a in range(5):
                        total[a] = total[a] + volume[d, a, b, chunk].astype(F32) * slope
            for a in range(5):
                xs[k + 1, a, chunk] = total[a]

        products(k, k + 1)
        arrive(0, k)
        arrive(1, k)
        arrive(2, k)

        @pl.when(k == 0)
        def _():
            from_neighbours()
            loads[10].wait()
            loads[11].wait()

        for s in range(2):
            for b in range(5):
                put_trace(6 + s, b, halo_x[k, s, b])
        gathered = jnp.dot(
            gather_left[:, 768:1024], pick_halo[...], preferred_element_type=F32
        )
        gathered = gathered[0:80] + gathered[80:160]
        rows[0] = rows[0] + gathered[:, 0:128]
        rows[1] = gathered[:, 128:256]
        for g in range(2):
            before = [rows[g, 16 * b : 16 * b + 16] for b in range(5)]
            for a in range(5):
                value = coupling[g, 5 * a : 5 * a + 1] * before[0]
                for b in range(1, 5):
                    row = 5 * a + b
                    value = value + coupling[g, row : row + 1] * before[b]
                rows[g, 16 * a : 16 * a + 16] = value
            nodes = [rows[g, pl.ds(m, 5, stride=16), :] for m in range(16)]
            for stage in range(2):
                after = [None] * 16
                for i in range(4):
                    for j in range(4):
                        own_index = i if stage == 0 else j
                        for m in range(4):
                            row = 16 * stage + 4 * own_index + m
                            node = 4 * m + j if stage == 0 else 4 * i + m
                            term = maps[g, row : row + 1] * nodes[node]
                            at = 4 * i + j
                            after[at] = term if m == 0 else after[at] + term
                nodes = after
            for m in range(16):
                rows[g, pl.ds(m, 5, stride=16), :] = nodes[m]
            high, low = split(rows[g])
            rows_left[0:80, g * LANES : (g + 1) * LANES] = high
            rows_left[80:160, g * LANES : (g + 1) * LANES] = low
        faces[...] = lax.dot_general(
            rows_left[...], place[...], (((1,), (1,)), ((), ())), preferred_element_type=F32
        )
        for f in range(6):
            d, s = f // 2, f % 2
            if d == 0:
                beside = [halo_x[k, s, b] for b in range(5)]
            elif d == 1:
                beside = [halo_y[k, s, b] for b in range(5)]
            else:
                edge = lane == (LANES - 1 if s == 0 else 0)
                turn = 1 if s == 0 else LANES - 1
                beside = [
                    pltpu.roll(
                        jnp.where(edge, halo_z[k, s, b], traces[k, 3 - s, b]), turn, 1
                    )
                    for b in range(5)
                ]
            columns = slice(f * LANES, (f + 1) * LANES)
            for a in range(5):
                value = (
                    faces[16 * a : 16 * a + 16, columns]
                    + faces[80 + 16 * a : 96 + 16 * a, columns]
                )
                for b in range(5):
                    value = value + surface[f, a, b].astype(F32) * beside[b]
                if d == 0:
                    at = 48 * s
                    xs[k + 1, a, at : at + 16] = xs[k + 1, a, at : at + 16] + value
                else:
                    high, low = split(value)
                    at = 16 * (f - 2)
                    faces_left[at : at + 16, a * LANES : (a + 1) * LANES] = high
                    faces_left[64 + at : 80 + at, a * LANES : (a + 1) * LANES] = low
        added = jnp.dot(back[...], faces_left[...], preferred_element_type=F32)
        for a in range(5):
            xs[k + 1, a] = xs[k + 1, a] + added[:, a * LANES : (a + 1) * LANES]

    products(KRYLOV, KRYLOV + 1)
    message[...] = lax.dot_general(
        jnp.ones((8, LANES), F32),
        gram[...],
        (((1,), (1,)), ((), ())),
        preferred_element_type=F32,
        precision=lax.Precision.HIGHEST,
    )

    def sum_copy(step):
        return pltpu.make_async_remote_copy(
            src_ref=message,
            dst_ref=messages.at[step],
            send_sem=sum_send.at[step],
            recv_sem=sum_recv.at[step],
            device_id=peer(step),
            device_id_type=MESH,
        )

    @pl.loop(1, group)
    def _(step):
        sum_copy(step).start()

    messages[0] = message[...]

    @pl.loop(1, group)
    def _(step):
        sum_copy(step).wait_recv()

    @pl.loop(1, group)
    def _(step):
        sum_copy(step).wait_send()

    def add(i, total):
        return total + messages[lax.rem(i + group - me, group)]

    total = lax.fori_loop(0, group, add, jnp.zeros((8, LANES), F32))
    size = KRYLOV + 1
    entries = [[None] * size for _ in range(size)]
    for k in range(size):
        for i in range(k + 1):
            entry = jnp.sum(jnp.where(lane == 8 * k + i, total, 0.0), axis=1, keepdims=True)
            entry = jnp.broadcast_to(entry, (8, LANES))
            entries[k][i] = entries[i][k] = entry
    scales = small_solve(entries)
    for b in range(5):
        for r in range(8):
            at = slice(8 * r, 8 * r + 8)
            value = scales[0] * xs[0, b, at]
            for k in range(1, KRYLOV):
                value = value + scales[k] * xs[k, b, at]
            out[b, at] = value


def local(
    sizes,
    adjoint_source,
    diagonal,
    volume_coupling,
    surface_coupling,
    mortar_owner,
    mortar_fine,
    mortar_coarse,
    mortar_quarter,
    mortar_side,
    mortar_coupling,
):
    forward, back = node_matrices()
    count = mortar_fine.shape[0]
    pairs = mortar_coupling.transpose(2, 3, 1, 0).reshape(25, 2, count)
    group = sizes[0] * sizes[1] * sizes[2]
    vmem = pl.BlockSpec(memory_space=pltpu.VMEM)
    dma = pltpu.SemaphoreType.DMA
    result = pl.pallas_call(
        functools.partial(kernel, sizes),
        out_shape=jax.ShapeDtypeStruct((5, 64, LANES), F32),
        in_specs=[pl.BlockSpec(memory_space=pltpu.HBM)] * 12,
        out_specs=vmem,
        scratch_shapes=[
            pltpu.VMEM((5, 64, LANES), BF16),
            pltpu.VMEM((3, 5, 5, 64, LANES), BF16),
            pltpu.VMEM((6, 5, 5, 16, LANES), BF16),
            pltpu.VMEM((5, 1, 64), jnp.int32),
            pltpu.VMEM((25, 2, 64), F32),
            pltpu.VMEM((256, 256), BF16),
            pltpu.VMEM((64, 128), BF16),
            pltpu.VMEM((32, LANES), F32),
            dma((12,)),
            pltpu.VMEM((KRYLOV + 1, 5, 64, LANES), F32),
            pltpu.VMEM((256, 5 * LANES), F32),
            pltpu.VMEM((256, 5 * LANES), BF16),
            pltpu.VMEM((KRYLOV, 4, 5, 16, LANES), F32),
            pltpu.VMEM((KRYLOV, 2, 5, 16, LANES), F32),
            pltpu.VMEM((KRYLOV, 2, 5, 16, LANES), F32),
            pltpu.VMEM((KRYLOV, 2, 5, 16, LANES), F32),
            pltpu.VMEM((2, 32, LANES), F32),
            pltpu.VMEM((160, 8 * LANES), BF16),
            pltpu.VMEM((6 * LANES, LANES), BF16),
            pltpu.VMEM((2 * LANES, 2 * LANES), BF16),
            pltpu.VMEM((6 * LANES, 2 * LANES), BF16),
            pltpu.VMEM((2, 32, LANES), F32),
            pltpu.VMEM((2, 32, LANES), F32),
            pltpu.VMEM((2, 80, LANES), F32),
            pltpu.VMEM((160, 2 * LANES), BF16),
            pltpu.VMEM((160, 6 * LANES), F32),
            pltpu.VMEM((128, 5 * LANES), BF16),
            pltpu.VMEM((LANES, LANES), F32),
            pltpu.VMEM((8, LANES), F32),
            pltpu.VMEM((group, 8, LANES), F32),
            dma((KRYLOV, 3, 2)),
            dma((KRYLOV, 3, 2)),
            dma((2,)),
            dma((2,)),
            dma((group,)),
            dma((group,)),
        ],
        compiler_params=pltpu.CompilerParams(
            collective_id=0, has_side_effects=True, vmem_limit_bytes=63 * 1024 * 1024
        ),
    )(
        adjoint_source.reshape(5, 64, LANES),
        diagonal.reshape(5, 64, LANES),
        volume_coupling.reshape(3, 5, 5, 64, LANES),
        surface_coupling.reshape(6, 5, 5, 16, LANES),
        mortar_owner.reshape(1, count),
        mortar_fine.reshape(1, count),
        mortar_coarse.reshape(1, count),
        mortar_quarter.reshape(1, count),
        mortar_side.reshape(1, count),
        pairs,
        jnp.asarray(forward),
        jnp.asarray(back),
    )
    return result.reshape(adjoint_source.shape)


def solution(mesh):
    placed = (
        P(None, None, None, None, ("groups", "gx"), "gy", "gz"),
        P(None, None, None, None, ("groups", "gx"), "gy", "gz"),
        P(None, None, None, None, None, None, ("groups", "gx"), "gy", "gz"),
        P(None, None, None, None, None, ("groups", "gx"), "gy", "gz"),
        P(("groups", "gx", "gy", "gz"), None),
        P(("groups", "gx", "gy", "gz")),
        P(("groups", "gx", "gy", "gz")),
        P(("groups", "gx", "gy", "gz")),
        P(("groups", "gx", "gy", "gz")),
        P(("groups", "gx", "gy", "gz"), None, None, None),
    )
    sizes = tuple(mesh.shape[a] for a in ("gx", "gy", "gz"))
    return jax.shard_map(
        functools.partial(local, sizes),
        mesh=mesh,
        in_specs=placed,
        out_specs=P(None, None, None, None, ("groups", "gx"), "gy", "gz"),
        check_vma=False,
    )
```

```python
import functools

import jax
import jax.numpy as jnp
import ml_dtypes
import numpy as np
from jax import lax
from jax.experimental import pallas as pl
from jax.experimental.pallas import tpu as pltpu
from jax.sharding import PartitionSpec as P

KRYLOV = 4
SHIFT = 3.0
F32 = jnp.float32
BF16 = jnp.bfloat16
LANES = 128
MESH = pl.DeviceIdType.MESH


def node_tables():
    points = np.array([-1.0, -1.0 / np.sqrt(5.0), 1.0 / np.sqrt(5.0), 1.0])
    barycentric = np.array(
        [1.0 / np.prod([points[m] - points[k] for k in range(4) if k != m]) for m in range(4)]
    )
    derivative = np.zeros((4, 4))
    for i in range(4):
        for m in range(4):
            if i != m:
                derivative[i, m] = barycentric[m] / barycentric[i] / (points[i] - points[m])
    for i in range(4):
        derivative[i, i] = -np.sum(derivative[i])
    halves = []
    for h in range(2):
        shifted = (points + 2 * h - 1) / 2.0
        lagrange = np.ones((4, 4))
        for m in range(4):
            for k in range(4):
                if k != m:
                    lagrange[:, m] = (
                        lagrange[:, m] * (shifted - points[k]) / (points[m] - points[k])
                    )
        halves.append(lagrange)
    return derivative.astype(np.float32), np.stack(halves).astype(np.float32)


def split(value):
    high = value.astype(BF16)
    return high, (value - high.astype(F32)).astype(BF16)


def node_matrices():
    derivative, _ = node_tables()
    eye = np.eye(4, dtype=np.float32)
    slopes = [
        np.kron(np.kron(derivative.T, eye), eye),
        np.kron(np.kron(eye, derivative.T), eye),
        np.kron(np.kron(eye, eye), derivative.T),
    ]
    traces = []
    for node in (0, 3):
        traces.append(np.kron(np.kron(eye, eye[node : node + 1]), eye))
    for node in (0, 3):
        traces.append(np.kron(np.kron(eye, eye), eye[node : node + 1]))
    traces = np.concatenate(traces)
    rows = np.concatenate(slopes)
    high = rows.astype(ml_dtypes.bfloat16)
    low = (rows - high.astype(np.float32)).astype(ml_dtypes.bfloat16)
    forward = np.concatenate([high, high, low, low], axis=1)
    back = np.concatenate([traces.T, traces.T], axis=1).astype(ml_dtypes.bfloat16)
    return forward, back


def small_solve(gram):
    size = KRYLOV + 1
    norm = jnp.sqrt(gram[0][0] + 1e-6)
    one = jnp.ones_like(norm)
    basis = [[one / norm]]
    images = [[gram[0][i] / norm for i in range(size)]]
    hess = [[None] * KRYLOV for _ in range(size)]
    for column in range(KRYLOV):
        current = basis[column]
        mapped = [SHIFT * c for c in current] + [None]
        for i, c in enumerate(current):
            mapped[i + 1] = c if mapped[i + 1] is None else mapped[i + 1] + c
        for earlier in range(column + 1):
            product = sum(m * images[earlier][i] for i, m in enumerate(mapped))
            hess[earlier][column] = product
            for i, c in enumerate(basis[earlier]):
                mapped[i] = mapped[i] - product * c
        image = [sum(m * gram[k][i] for k, m in enumerate(mapped)) for i in range(size)]
        square = sum(m * image[i] for i, m in enumerate(mapped))
        length = jnp.sqrt(jnp.maximum(square, 0.0) + 1e-6)
        hess[column + 1][column] = length
        if column + 1 < KRYLOV:
            scale = one / length
            basis.append([m * scale for m in mapped])
            images.append([m * scale for m in image])
    normal = [[None] * KRYLOV for _ in range(KRYLOV)]
    for i in range(KRYLOV):
        for j in range(i + 1):
            normal[i][j] = sum(hess[r][i] * hess[r][j] for r in range(j + 2))
    factor = [[None] * KRYLOV for _ in range(KRYLOV)]
    inverse = [None] * KRYLOV
    for j in range(KRYLOV):
        pivot = normal[j][j]
        for k in range(j):
            pivot = pivot - factor[j][k] * factor[j][k]
        factor[j][j] = jnp.sqrt(pivot)
        inverse[j] = one / factor[j][j]
        for i in range(j + 1, KRYLOV):
            value = normal[i][j]
            for k in range(j):
                value = value - factor[i][k] * factor[j][k]
            factor[i][j] = value * inverse[j]
    half = []
    for i in range(KRYLOV):
        value = norm * hess[0][i]
        for k in range(i):
            value = value - factor[i][k] * half[k]
        half.append(value * inverse[i])
    weights = [None] * KRYLOV
    for i in reversed(range(KRYLOV)):
        value = half[i]
        for k in range(i + 1, KRYLOV):
            value = value - factor[k][i] * weights[k]
        weights[i] = value * inverse[i]
    return [
        sum(weights[j] * basis[j][i] for j in range(i, KRYLOV)) for i in range(KRYLOV)
    ]


def kernel(
    sizes,
    source_hbm,
    diagonal_hbm,
    volume_hbm,
    surface_hbm,
    owner_hbm,
    fine_hbm,
    coarse_hbm,
    quarter_hbm,
    side_hbm,
    coupling_hbm,
    forward_hbm,
    back_hbm,
    out,
    diagonal,
    volume,
    surface,
    numbers,
    pairs,
    forward,
    back,
    pack,
    load_sem,
    xs,
    slopes,
    right,
    traces,
    halo_x,
    halo_y,
    halo_z,
    neighbour_pack,
    gather_left,
    pick_own,
    pick_halo,
    place,
    coupling,
    maps,
    rows,
    rows_left,
    faces,
    faces_left,
    gram,
    message,
    messages,
    send_sem,
    recv_sem,
    pack_send,
    pack_recv,
    sum_send,
    sum_recv,
):
    axes = ("gx", "gy", "gz")
    here = [lax.axis_index(a) for a in axes]
    group = sizes[0] * sizes[1] * sizes[2]
    me = (here[0] * sizes[1] + here[1]) * sizes[2] + here[2]
    has_low = [h > 0 for h in here]
    has_high = [h < n - 1 for h, n in zip(here, sizes)]

    def peer(step):
        other = lax.rem(me + step, group)
        return {
            "gx": other // (sizes[1] * sizes[2]),
            "gy": lax.rem(other // sizes[2], sizes[1]),
            "gz": lax.rem(other, sizes[2]),
        }

    barrier = pltpu.get_barrier_semaphore()

    @pl.loop(1, group)
    def _(step):
        pl.semaphore_signal(barrier, inc=1, device_id=peer(step), device_id_type=MESH)

    loads = [
        pltpu.make_async_copy(origin, target, load_sem.at[i])
        for i, (origin, target) in enumerate(
            (
                (source_hbm, xs.at[0]),
                (owner_hbm, numbers.at[0]),
                (fine_hbm, numbers.at[1]),
                (coarse_hbm, numbers.at[2]),
                (quarter_hbm, numbers.at[3]),
                (side_hbm, numbers.at[4]),
                (coupling_hbm, pairs),
                (forward_hbm, forward),
                (diagonal_hbm, diagonal),
                (volume_hbm, volume),
                (surface_hbm, surface),
                (back_hbm, back),
            )
        )
    ]
    for load in loads:
        load.start()

    halos = (halo_x, halo_y, halo_z)
    for d in range(3):
        for s, there in ((0, has_low[d]), (1, has_high[d])):

            @pl.when(jnp.logical_not(there))
            def _(d=d, s=s):
                for k in range(KRYLOV):
                    halos[d][k, s] = jnp.zeros((5, 16, LANES), F32)

                if d == 0:
                    neighbour_pack[s] = jnp.full((32, LANES), -9.0, F32)

    for load in loads[1:7]:
        load.wait()
    for half in range(2):
        at = slice(64 * half, 64 * half + 64)
        pack[0:25, at] = pairs[:, half, :]
        for i in range(5):
            pack[25 + i : 26 + i, at] = numbers[i].astype(F32)
    pack[30:32] = jnp.zeros((2, LANES), F32)
    pl.semaphore_wait(barrier, group - 1)

    def to(d, s):
        return {axes[d]: here[d] - 1 if s == 0 else here[d] + 1}

    def pack_copy(s):
        return pltpu.make_async_remote_copy(
            src_ref=pack,
            dst_ref=neighbour_pack.at[1 - s],
            send_sem=pack_send.at[s],
            recv_sem=pack_recv.at[s],
            device_id=to(0, s),
            device_id_type=MESH,
        )

    def face_copy(d, s, k):
        if d == 0:
            face = xs.at[k, :, pl.ds(48 * s, 16), :]
        else:
            face = traces.at[k, 2 * (d - 1) + s]
        return pltpu.make_async_remote_copy(
            src_ref=face,
            dst_ref=halos[d].at[k, 1 - s],
            send_sem=send_sem.at[k, d, s],
            recv_sem=recv_sem.at[k, d, s],
            device_id=to(d, s),
            device_id_type=MESH,
        )

    def sides(d, s):
        return (has_low[d], has_high[d]) if s == 0 else (has_high[d], has_low[d])

    def start(d, k):
        for s in range(2):
            target, _ = sides(d, s)

            @pl.when(target)
            def _(s=s):
                face_copy(d, s, k).start()

    def arrive(d, k):
        for s in range(2):
            target, origin = sides(d, s)

            @pl.when(origin)
            def _(s=s):
                face_copy(d, s, k).wait_recv()

            @pl.when(target)
            def _(s=s):
                face_copy(d, s, k).wait_send()

    for s in range(2):

        @pl.when(sides(0, s)[0])
        def _(s=s):
            pack_copy(s).start()

    lane = lax.broadcasted_iota(jnp.int32, (1, LANES), 1)
    left_half = lane < 64
    _, halves = node_tables()

    def keys(packed, me_x):
        offset = packed[25:26] - me_x
        fine, coarse, quarter, side = (packed[r : r + 1] for r in range(26, 30))
        odd = jnp.floor(side * 0.5)
        opposite = side + 1.0 - 2.0 * (side - 2.0 * odd)
        return offset, fine, coarse, quarter, side, opposite

    def one_hot(key, count):
        index = lax.broadcasted_iota(jnp.int32, (count, LANES), 0).astype(F32)
        return jnp.where(index == key, 1.0, 0.0).astype(BF16)

    def make_maps(slot, quarter, flipped):
        first = quarter >= 2.0
        second = (quarter - 2.0 * jnp.where(first, 1.0, 0.0)) >= 1.0
        for stage, bit in ((0, first), (1, second)):
            for i in range(4):
                for m in range(4):
                    straight = jnp.where(bit, float(halves[1, i, m]), float(halves[0, i, m]))
                    turned = jnp.where(bit, float(halves[1, m, i]), float(halves[0, m, i]))
                    row = 16 * stage + 4 * i + m
                    maps[slot, row : row + 1] = jnp.where(flipped, turned, straight)

    place_x = here[0].astype(F32)

    def from_own():
        own = pack[...]
        offset, fine, coarse, quarter, side, opposite = keys(own, place_x)
        same = offset == 0.0
        at_coarse = jnp.where(same, opposite * LANES + coarse, -1.0)
        at_fine = side * LANES + fine
        pick_own[...] = one_hot(
            jnp.where(left_half, at_coarse, jnp.where(same, at_fine, -1.0)), 768
        )
        outside = jnp.where(offset < 0.0, coarse, LANES + coarse)
        pick_halo[:, 0:128] = one_hot(
            jnp.where(left_half & jnp.logical_not(same), outside, -1.0), 256
        )
        place[:, 0:128] = one_hot(jnp.where(left_half, at_fine, at_coarse), 768)
        coupling[0] = own
        make_maps(0, quarter, jnp.logical_not(left_half))

    def from_neighbours():
        for s in range(2):
            target, origin = sides(0, s)

            @pl.when(origin)
            def _(s=s):
                pack_copy(s).wait_recv()

            @pl.when(target)
            def _(s=s):
                pack_copy(s).wait_send()

        both = jnp.where(left_half, pltpu.roll(neighbour_pack[0], 64, 1), neighbour_pack[1])
        offset, fine, coarse, quarter, _, _ = keys(both, place_x)
        valid = offset == 0.0
        base = jnp.where(left_half, 0.0, 1.0 * LANES)
        pick_halo[:, 128:256] = one_hot(jnp.where(valid, base + fine, -1.0), 256)
        place[:, 128:256] = one_hot(jnp.where(valid, base + coarse, -1.0), 768)
        coupling[1] = jnp.where(valid, both, 0.0)
        make_maps(1, jnp.where(valid, quarter, 0.0), lane >= 0)

    def put_trace(block, var, value):
        high, low = split(value)
        columns = pl.ds(block * LANES, LANES)
        gather_left[pl.ds(16 * var, 16), columns] = high
        gather_left[pl.ds(80 + 16 * var, 16), columns] = low

    def products(k, count):
        @pl.loop(0, count)
        def _(i):
            total = jnp.zeros((8, LANES), F32)
            for b in range(5):
                both = xs[k, b] * xs[i, b]
                for r in range(8):
                    total = total + both[8 * r : 8 * r + 8]
            gram[pl.ds(k * 8 + i, 1), :] = jnp.sum(total, axis=0, keepdims=True)

    gram[...] = jnp.zeros_like(gram)
    loads[0].wait()

    @pl.loop(0, KRYLOV)
    def _(k):
        start(0, k)
        for s in range(2):
            for b in range(5):
                for i in range(4):
                    at = 16 * i + 12 * s
                    traces[k, s, b, 4 * i : 4 * i + 4] = xs[k, b, at : at + 4]
        start(1, k)
        for s in range(2):
            for b in range(5):
                traces[k, 2 + s, b] = xs[k, b, pl.ds(3 * s, 16, stride=4), :]
        start(2, k)
        for b in range(5):
            high, low = split(xs[k, b])
            columns = slice(b * LANES, (b + 1) * LANES)
            right[0:64, columns] = high
            right[64:128, columns] = low
            right[128:192, columns] = high
            right[192:256, columns] = low

        @pl.when(k == 0)
        def _():
            loads[7].wait()

        slopes[...] = jnp.dot(forward[...], right[...], preferred_element_type=F32)

        @pl.when(k == 0)
        def _():
            from_own()
            loads[8].wait()
            loads[9].wait()

        for b in range(5):
            put_trace(0, b, xs[k, b, 0:16])
            put_trace(1, b, xs[k, b, 48:64])
            for f in range(4):
                put_trace(2 + f, b, traces[k, f, b])
        gathered = jnp.dot(
            gather_left[:, 0:768], pick_own[...], preferred_element_type=F32
        )
        rows[0] = gathered[0:80] + gathered[80:160]

        @pl.loop(0, 4)
        def _(c):
            chunk = pl.ds(pl.multiple_of(16 * c, 16), 16)
            total = [
                (diagonal[a, chunk].astype(F32) - SHIFT) * xs[k, a, chunk] for a in range(5)
            ]
            for d in range(3):
                for b in range(5):
                    slope = slopes[
                        pl.ds(pl.multiple_of(64 * d + 16 * c, 16), 16),
                        b * LANES : (b + 1) * LANES,
                    ]
                    for a in range(5):
                        total[a] = total[a] + volume[d, a, b, chunk].astype(F32) * slope
            for a in range(5):
                xs[k + 1, a, chunk] = total[a]

        products(k, k + 1)

        @pl.when(k == 0)
        def _():
            from_neighbours()
            loads[10].wait()
            loads[11].wait()

        arrive(0, k)
        arrive(1, k)
        arrive(2, k)
        for s in range(2):
            for b in range(5):
                put_trace(6 + s, b, halo_x[k, s, b])
        gathered = jnp.dot(
            gather_left[:, 768:1024], pick_halo[...], preferred_element_type=F32
        )
        gathered = gathered[0:80] + gathered[80:160]
        rows[0] = rows[0] + gathered[:, 0:128]
        rows[1] = gathered[:, 128:256]
        for g in range(2):
            before = [rows[g, 16 * b : 16 * b + 16] for b in range(5)]
            for a in range(5):
                value = coupling[g, 5 * a : 5 * a + 1] * before[0]
                for b in range(1, 5):
                    row = 5 * a + b
                    value = value + coupling[g, row : row + 1] * before[b]
                rows[g, 16 * a : 16 * a + 16] = value
            nodes = [rows[g, pl.ds(m, 5, stride=16), :] for m in range(16)]
            for stage in range(2):
                after = [None] * 16
                for i in range(4):
                    for j in range(4):
                        own_index = i if stage == 0 else j
                        for m in range(4):
                            row = 16 * stage + 4 * own_index + m
                            node = 4 * m + j if stage == 0 else 4 * i + m
                            term = maps[g, row : row + 1] * nodes[node]
                            at = 4 * i + j
                            after[at] = term if m == 0 else after[at] + term
                nodes = after
            for m in range(16):
                rows[g, pl.ds(m, 5, stride=16), :] = nodes[m]
            high, low = split(rows[g])
            rows_left[0:80, g * LANES : (g + 1) * LANES] = high
            rows_left[80:160, g * LANES : (g + 1) * LANES] = low
        faces[...] = lax.dot_general(
            rows_left[...], place[...], (((1,), (1,)), ((), ())), preferred_element_type=F32
        )
        for f in range(6):
            d, s = f // 2, f % 2
            if d == 0:
                beside = [halo_x[k, s, b] for b in range(5)]
            elif d == 1:
                beside = [halo_y[k, s, b] for b in range(5)]
            else:
                edge = lane == (LANES - 1 if s == 0 else 0)
                turn = 1 if s == 0 else LANES - 1
                beside = [
                    pltpu.roll(
                        jnp.where(edge, halo_z[k, s, b], traces[k, 3 - s, b]), turn, 1
                    )
                    for b in range(5)
                ]
            columns = slice(f * LANES, (f + 1) * LANES)
            for a in range(5):
                value = (
                    faces[16 * a : 16 * a + 16, columns]
                    + faces[80 + 16 * a : 96 + 16 * a, columns]
                )
                for b in range(5):
                    value = value + surface[f, a, b].astype(F32) * beside[b]
                if d == 0:
                    at = 48 * s
                    xs[k + 1, a, at : at + 16] = xs[k + 1, a, at : at + 16] + value
                else:
                    high, low = split(value)
                    at = 16 * (f - 2)
                    faces_left[at : at + 16, a * LANES : (a + 1) * LANES] = high
                    faces_left[64 + at : 80 + at, a * LANES : (a + 1) * LANES] = low
        added = jnp.dot(back[...], faces_left[...], preferred_element_type=F32)
        for a in range(5):
            xs[k + 1, a] = xs[k + 1, a] + added[:, a * LANES : (a + 1) * LANES]

    products(KRYLOV, KRYLOV + 1)
    sums = lax.dot_general(
        jnp.ones((8, LANES), F32),
        gram[...],
        (((1,), (1,)), ((), ())),
        preferred_element_type=F32,
        precision=lax.Precision.HIGHEST,
    )
    message[...] = sums[0:1]

    def sum_copy(step):
        return pltpu.make_async_remote_copy(
            src_ref=message,
            dst_ref=messages.at[step],
            send_sem=sum_send.at[step],
            recv_sem=sum_recv.at[step],
            device_id=peer(step),
            device_id_type=MESH,
        )

    @pl.loop(1, group)
    def _(step):
        sum_copy(step).start()

    messages[0] = message[...]

    @pl.loop(1, group)
    def _(step):
        sum_copy(step).wait_recv()

    @pl.loop(1, group)
    def _(step):
        sum_copy(step).wait_send()

    def add(i, total):
        return total + messages[lax.rem(i + group - me, group)]

    total = lax.fori_loop(0, group, add, jnp.zeros((1, LANES), F32))
    size = KRYLOV + 1
    entries = [[None] * size for _ in range(size)]
    for k in range(size):
        for i in range(k + 1):
            entry = jnp.sum(jnp.where(lane == 8 * k + i, total, 0.0), axis=1, keepdims=True)
            entry = jnp.broadcast_to(entry, (8, LANES))
            entries[k][i] = entries[i][k] = entry
    scales = small_solve(entries)
    for b in range(5):
        for r in range(8):
            at = slice(8 * r, 8 * r + 8)
            value = scales[0] * xs[0, b, at]
            for k in range(1, KRYLOV):
                value = value + scales[k] * xs[k, b, at]
            out[b, at] = value


def local(
    sizes,
    adjoint_source,
    diagonal,
    volume_coupling,
    surface_coupling,
    mortar_owner,
    mortar_fine,
    mortar_coarse,
    mortar_quarter,
    mortar_side,
    mortar_coupling,
):
    forward, back = node_matrices()
    count = mortar_fine.shape[0]
    pairs = mortar_coupling.transpose(2, 3, 1, 0).reshape(25, 2, count)
    group = sizes[0] * sizes[1] * sizes[2]
    vmem = pl.BlockSpec(memory_space=pltpu.VMEM)
    dma = pltpu.SemaphoreType.DMA
    result = pl.pallas_call(
        functools.partial(kernel, sizes),
        out_shape=jax.ShapeDtypeStruct((5, 64, LANES), F32),
        in_specs=[pl.BlockSpec(memory_space=pltpu.HBM)] * 12,
        out_specs=vmem,
        scratch_shapes=[
            pltpu.VMEM((5, 64, LANES), BF16),
            pltpu.VMEM((3, 5, 5, 64, LANES), BF16),
            pltpu.VMEM((6, 5, 5, 16, LANES), BF16),
            pltpu.VMEM((5, 1, 64), jnp.int32),
            pltpu.VMEM((25, 2, 64), F32),
            pltpu.VMEM((192, 256), BF16),
            pltpu.VMEM((64, 128), BF16),
            pltpu.VMEM((32, LANES), F32),
            dma((12,)),
            pltpu.VMEM((KRYLOV + 1, 5, 64, LANES), F32),
            pltpu.VMEM((192, 5 * LANES), F32),
            pltpu.VMEM((256, 5 * LANES), BF16),
            pltpu.VMEM((KRYLOV, 4, 5, 16, LANES), F32),
            pltpu.VMEM((KRYLOV, 2, 5, 16, LANES), F32),
            pltpu.VMEM((KRYLOV, 2, 5, 16, LANES), F32),
            pltpu.VMEM((KRYLOV, 2, 5, 16, LANES), F32),
            pltpu.VMEM((2, 32, LANES), F32),
            pltpu.VMEM((160, 8 * LANES), BF16),
            pltpu.VMEM((6 * LANES, LANES), BF16),
            pltpu.VMEM((2 * LANES, 2 * LANES), BF16),
            pltpu.VMEM((6 * LANES, 2 * LANES), BF16),
            pltpu.VMEM((2, 32, LANES), F32),
            pltpu.VMEM((2, 32, LANES), F32),
            pltpu.VMEM((2, 80, LANES), F32),
            pltpu.VMEM((160, 2 * LANES), BF16),
            pltpu.VMEM((160, 6 * LANES), F32),
            pltpu.VMEM((128, 5 * LANES), BF16),
            pltpu.VMEM((LANES, LANES), F32),
            pltpu.VMEM((1, LANES), F32),
            pltpu.VMEM((group, 1, LANES), F32),
            dma((KRYLOV, 3, 2)),
            dma((KRYLOV, 3, 2)),
            dma((2,)),
            dma((2,)),
            dma((group,)),
            dma((group,)),
        ],
        compiler_params=pltpu.CompilerParams(
            collective_id=0, has_side_effects=True, vmem_limit_bytes=63 * 1024 * 1024
        ),
    )(
        adjoint_source.reshape(5, 64, LANES),
        diagonal.reshape(5, 64, LANES),
        volume_coupling.reshape(3, 5, 5, 64, LANES),
        surface_coupling.reshape(6, 5, 5, 16, LANES),
        mortar_owner.reshape(1, count),
        mortar_fine.reshape(1, count),
        mortar_coarse.reshape(1, count),
        mortar_quarter.reshape(1, count),
        mortar_side.reshape(1, count),
        pairs,
        jnp.asarray(forward),
        jnp.asarray(back),
    )
    return result.reshape(adjoint_source.shape)


def solution(mesh):
    placed = (
        P(None, None, None, None, ("groups", "gx"), "gy", "gz"),
        P(None, None, None, None, ("groups", "gx"), "gy", "gz"),
        P(None, None, None, None, None, None, ("groups", "gx"), "gy", "gz"),
        P(None, None, None, None, None, ("groups", "gx"), "gy", "gz"),
        P(("groups", "gx", "gy", "gz"), None),
        P(("groups", "gx", "gy", "gz")),
        P(("groups", "gx", "gy", "gz")),
        P(("groups", "gx", "gy", "gz")),
        P(("groups", "gx", "gy", "gz")),
        P(("groups", "gx", "gy", "gz"), None, None, None),
    )
    sizes = tuple(mesh.shape[a] for a in ("gx", "gy", "gz"))
    return jax.shard_map(
        functools.partial(local, sizes),
        mesh=mesh,
        in_specs=placed,
        out_specs=P(None, None, None, None, ("groups", "gx"), "gy", "gz"),
        check_vma=False,
    )
```

```python
import functools

import jax
import jax.numpy as jnp
import ml_dtypes
import numpy as np
from jax import lax
from jax.experimental import pallas as pl
from jax.experimental.pallas import tpu as pltpu
from jax.sharding import PartitionSpec as P

KRYLOV = 4
SHIFT = 3.0
F32 = jnp.float32
BF16 = jnp.bfloat16
LANES = 128
MESH = pl.DeviceIdType.MESH


def node_tables():
    points = np.array([-1.0, -1.0 / np.sqrt(5.0), 1.0 / np.sqrt(5.0), 1.0])
    barycentric = np.array(
        [1.0 / np.prod([points[m] - points[k] for k in range(4) if k != m]) for m in range(4)]
    )
    derivative = np.zeros((4, 4))
    for i in range(4):
        for m in range(4):
            if i != m:
                derivative[i, m] = barycentric[m] / barycentric[i] / (points[i] - points[m])
    for i in range(4):
        derivative[i, i] = -np.sum(derivative[i])
    halves = []
    for h in range(2):
        shifted = (points + 2 * h - 1) / 2.0
        lagrange = np.ones((4, 4))
        for m in range(4):
            for k in range(4):
                if k != m:
                    lagrange[:, m] = (
                        lagrange[:, m] * (shifted - points[k]) / (points[m] - points[k])
                    )
        halves.append(lagrange)
    return derivative.astype(np.float32), np.stack(halves).astype(np.float32)


def split(value):
    high = value.astype(BF16)
    return high, (value - high.astype(F32)).astype(BF16)


def node_matrices():
    derivative, _ = node_tables()
    eye = np.eye(4, dtype=np.float32)
    slopes = [
        np.kron(np.kron(derivative.T, eye), eye),
        np.kron(np.kron(eye, derivative.T), eye),
        np.kron(np.kron(eye, eye), derivative.T),
    ]
    traces = []
    for node in (0, 3):
        traces.append(np.kron(np.kron(eye, eye[node : node + 1]), eye))
    for node in (0, 3):
        traces.append(np.kron(np.kron(eye, eye), eye[node : node + 1]))
    traces = np.concatenate(traces)
    rows = np.concatenate(slopes)
    high = rows.astype(ml_dtypes.bfloat16)
    low = (rows - high.astype(np.float32)).astype(ml_dtypes.bfloat16)
    forward = np.concatenate([high, high, low, low], axis=1)
    back = np.concatenate([traces.T, traces.T], axis=1).astype(ml_dtypes.bfloat16)
    return forward, back


def small_solve(gram):
    size = KRYLOV + 1
    norm = jnp.sqrt(gram[0][0] + 1e-6)
    one = jnp.ones_like(norm)
    basis = [[one / norm]]
    images = [[gram[0][i] / norm for i in range(size)]]
    hess = [[None] * KRYLOV for _ in range(size)]
    for column in range(KRYLOV):
        current = basis[column]
        mapped = [SHIFT * c for c in current] + [None]
        for i, c in enumerate(current):
            mapped[i + 1] = c if mapped[i + 1] is None else mapped[i + 1] + c
        for earlier in range(column + 1):
            product = sum(m * images[earlier][i] for i, m in enumerate(mapped))
            hess[earlier][column] = product
            for i, c in enumerate(basis[earlier]):
                mapped[i] = mapped[i] - product * c
        image = [sum(m * gram[k][i] for k, m in enumerate(mapped)) for i in range(size)]
        square = sum(m * image[i] for i, m in enumerate(mapped))
        length = jnp.sqrt(jnp.maximum(square, 0.0) + 1e-6)
        hess[column + 1][column] = length
        if column + 1 < KRYLOV:
            scale = one / length
            basis.append([m * scale for m in mapped])
            images.append([m * scale for m in image])
    normal = [[None] * KRYLOV for _ in range(KRYLOV)]
    for i in range(KRYLOV):
        for j in range(i + 1):
            normal[i][j] = sum(hess[r][i] * hess[r][j] for r in range(j + 2))
    factor = [[None] * KRYLOV for _ in range(KRYLOV)]
    inverse = [None] * KRYLOV
    for j in range(KRYLOV):
        pivot = normal[j][j]
        for k in range(j):
            pivot = pivot - factor[j][k] * factor[j][k]
        factor[j][j] = jnp.sqrt(pivot)
        inverse[j] = one / factor[j][j]
        for i in range(j + 1, KRYLOV):
            value = normal[i][j]
            for k in range(j):
                value = value - factor[i][k] * factor[j][k]
            factor[i][j] = value * inverse[j]
    half = []
    for i in range(KRYLOV):
        value = norm * hess[0][i]
        for k in range(i):
            value = value - factor[i][k] * half[k]
        half.append(value * inverse[i])
    weights = [None] * KRYLOV
    for i in reversed(range(KRYLOV)):
        value = half[i]
        for k in range(i + 1, KRYLOV):
            value = value - factor[k][i] * weights[k]
        weights[i] = value * inverse[i]
    return [
        sum(weights[j] * basis[j][i] for j in range(i, KRYLOV)) for i in range(KRYLOV)
    ]


def kernel(
    sizes,
    source_hbm,
    diagonal_hbm,
    volume_hbm,
    surface_hbm,
    owner_hbm,
    fine_hbm,
    coarse_hbm,
    quarter_hbm,
    side_hbm,
    coupling_hbm,
    forward_hbm,
    back_hbm,
    out,
    diagonal,
    volume,
    surface,
    numbers,
    pairs,
    forward,
    back,
    pack,
    load_sem,
    xs,
    slopes,
    right,
    traces,
    halo_x,
    halo_y,
    halo_z,
    neighbour_pack,
    gather_left,
    pick_own,
    pick_halo,
    place,
    coupling,
    maps,
    rows,
    rows_left,
    faces,
    faces_left,
    gram,
    message,
    messages,
    send_sem,
    recv_sem,
    pack_send,
    pack_recv,
    sum_send,
    sum_recv,
):
    axes = ("gx", "gy", "gz")
    here = [lax.axis_index(a) for a in axes]
    group = sizes[0] * sizes[1] * sizes[2]
    me = (here[0] * sizes[1] + here[1]) * sizes[2] + here[2]
    has_low = [h > 0 for h in here]
    has_high = [h < n - 1 for h, n in zip(here, sizes)]

    def wrapped(value, size):
        return jnp.where(value >= size, value - size, value)

    def each(action):
        if group > 16:
            pl.loop(1, group)(action)
        else:
            for step in range(1, group):
                action(step)

    def peer(step):
        if isinstance(step, int):
            steps = (step // (sizes[1] * sizes[2]), step // sizes[2] % sizes[1], step % sizes[2])
            return {a: wrapped(h + o, n) for a, h, o, n in zip(axes, here, steps, sizes)}
        other = lax.rem(me + step, group)
        return {
            "gx": other // (sizes[1] * sizes[2]),
            "gy": lax.rem(other // sizes[2], sizes[1]),
            "gz": lax.rem(other, sizes[2]),
        }

    barrier = pltpu.get_barrier_semaphore()

    each(
        lambda step: pl.semaphore_signal(
            barrier, inc=1, device_id=peer(step), device_id_type=MESH
        )
    )

    loads = [
        pltpu.make_async_copy(origin, target, load_sem.at[i])
        for i, (origin, target) in enumerate(
            (
                (source_hbm, xs.at[0]),
                (owner_hbm, numbers.at[0]),
                (fine_hbm, numbers.at[1]),
                (coarse_hbm, numbers.at[2]),
                (quarter_hbm, numbers.at[3]),
                (side_hbm, numbers.at[4]),
                (coupling_hbm, pairs),
                (forward_hbm, forward),
                (diagonal_hbm, diagonal),
                (volume_hbm, volume),
                (surface_hbm, surface),
                (back_hbm, back),
            )
        )
    ]
    for load in loads:
        load.start()

    halos = (halo_x, halo_y, halo_z)
    for d in range(3):
        for s, there in ((0, has_low[d]), (1, has_high[d])):

            @pl.when(jnp.logical_not(there))
            def _(d=d, s=s):
                for k in range(KRYLOV):
                    halos[d][k, s] = jnp.zeros((5, 16, LANES), F32)

                if d == 0:
                    neighbour_pack[s] = jnp.full((32, LANES), -9.0, F32)

    for load in loads[1:7]:
        load.wait()
    for half in range(2):
        at = slice(64 * half, 64 * half + 64)
        pack[0:25, at] = pairs[:, half, :]
        for i in range(5):
            pack[25 + i : 26 + i, at] = numbers[i].astype(F32)
    pack[30:32] = jnp.zeros((2, LANES), F32)
    pl.semaphore_wait(barrier, group - 1)

    def to(d, s):
        return {axes[d]: here[d] - 1 if s == 0 else here[d] + 1}

    def pack_copy(s):
        return pltpu.make_async_remote_copy(
            src_ref=pack,
            dst_ref=neighbour_pack.at[1 - s],
            send_sem=pack_send.at[s],
            recv_sem=pack_recv.at[s],
            device_id=to(0, s),
            device_id_type=MESH,
        )

    def face_copy(d, s, k):
        if d == 0:
            face = xs.at[k, :, pl.ds(48 * s, 16), :]
        else:
            face = traces.at[k, 2 * (d - 1) + s]
        return pltpu.make_async_remote_copy(
            src_ref=face,
            dst_ref=halos[d].at[k, 1 - s],
            send_sem=send_sem.at[k, d, s],
            recv_sem=recv_sem.at[k, d, s],
            device_id=to(d, s),
            device_id_type=MESH,
        )

    def sides(d, s):
        return (has_low[d], has_high[d]) if s == 0 else (has_high[d], has_low[d])

    def start(d, k):
        for s in range(2):
            target, _ = sides(d, s)

            @pl.when(target)
            def _(s=s):
                face_copy(d, s, k).start()

    def arrive(d, k):
        for s in range(2):
            target, origin = sides(d, s)

            @pl.when(origin)
            def _(s=s):
                face_copy(d, s, k).wait_recv()

            @pl.when(target)
            def _(s=s):
                face_copy(d, s, k).wait_send()

    for s in range(2):

        @pl.when(sides(0, s)[0])
        def _(s=s):
            pack_copy(s).start()

    lane = lax.broadcasted_iota(jnp.int32, (1, LANES), 1)
    left_half = lane < 64
    _, halves = node_tables()

    def keys(packed, me_x):
        offset = packed[25:26] - me_x
        fine, coarse, quarter, side = (packed[r : r + 1] for r in range(26, 30))
        odd = jnp.floor(side * 0.5)
        opposite = side + 1.0 - 2.0 * (side - 2.0 * odd)
        return offset, fine, coarse, quarter, side, opposite

    def one_hot(key, count):
        index = lax.broadcasted_iota(jnp.int32, (count, LANES), 0).astype(F32)
        return jnp.where(index == key, 1.0, 0.0).astype(BF16)

    def make_maps(slot, quarter, flipped):
        first = quarter >= 2.0
        second = (quarter - 2.0 * jnp.where(first, 1.0, 0.0)) >= 1.0
        for stage, bit in ((0, first), (1, second)):
            for i in range(4):
                for m in range(4):
                    straight = jnp.where(bit, float(halves[1, i, m]), float(halves[0, i, m]))
                    turned = jnp.where(bit, float(halves[1, m, i]), float(halves[0, m, i]))
                    row = 16 * stage + 4 * i + m
                    maps[slot, row : row + 1] = jnp.where(flipped, turned, straight)

    place_x = here[0].astype(F32)

    def from_own():
        own = pack[...]
        offset, fine, coarse, quarter, side, opposite = keys(own, place_x)
        same = offset == 0.0
        at_coarse = jnp.where(same, opposite * LANES + coarse, -1.0)
        at_fine = side * LANES + fine
        pick_own[...] = one_hot(
            jnp.where(left_half, at_coarse, jnp.where(same, at_fine, -1.0)), 768
        )
        outside = jnp.where(offset < 0.0, coarse, LANES + coarse)
        pick_halo[:, 0:128] = one_hot(
            jnp.where(left_half & jnp.logical_not(same), outside, -1.0), 256
        )
        place[:, 0:128] = one_hot(jnp.where(left_half, at_fine, at_coarse), 768)
        coupling[0] = own
        make_maps(0, quarter, jnp.logical_not(left_half))

    def from_neighbours():
        for s in range(2):
            target, origin = sides(0, s)

            @pl.when(origin)
            def _(s=s):
                pack_copy(s).wait_recv()

            @pl.when(target)
            def _(s=s):
                pack_copy(s).wait_send()

        both = jnp.where(left_half, pltpu.roll(neighbour_pack[0], 64, 1), neighbour_pack[1])
        offset, fine, coarse, quarter, _, _ = keys(both, place_x)
        valid = offset == 0.0
        base = jnp.where(left_half, 0.0, 1.0 * LANES)
        pick_halo[:, 128:256] = one_hot(jnp.where(valid, base + fine, -1.0), 256)
        place[:, 128:256] = one_hot(jnp.where(valid, base + coarse, -1.0), 768)
        coupling[1] = jnp.where(valid, both, 0.0)
        make_maps(1, jnp.where(valid, quarter, 0.0), lane >= 0)

    def put_trace(block, var, value):
        high, low = split(value)
        columns = pl.ds(block * LANES, LANES)
        gather_left[pl.ds(16 * var, 16), columns] = high
        gather_left[pl.ds(80 + 16 * var, 16), columns] = low

    def products(k, count):
        @pl.loop(0, count)
        def _(i):
            total = jnp.zeros((8, LANES), F32)
            for b in range(5):
                both = xs[k, b] * xs[i, b]
                for r in range(8):
                    total = total + both[8 * r : 8 * r + 8]
            gram[pl.ds(k * 8 + i, 1), :] = jnp.sum(total, axis=0, keepdims=True)

    gram[...] = jnp.zeros_like(gram)
    loads[0].wait()

    @pl.loop(0, KRYLOV)
    def _(k):
        start(0, k)
        for s in range(2):
            for b in range(5):
                for i in range(4):
                    at = 16 * i + 12 * s
                    traces[k, s, b, 4 * i : 4 * i + 4] = xs[k, b, at : at + 4]
        start(1, k)
        for s in range(2):
            for b in range(5):
                traces[k, 2 + s, b] = xs[k, b, pl.ds(3 * s, 16, stride=4), :]
        start(2, k)
        for b in range(5):
            high, low = split(xs[k, b])
            columns = slice(b * LANES, (b + 1) * LANES)
            right[0:64, columns] = high
            right[64:128, columns] = low
            right[128:192, columns] = high
            right[192:256, columns] = low

        @pl.when(k == 0)
        def _():
            loads[7].wait()

        slopes[...] = jnp.dot(forward[...], right[...], preferred_element_type=F32)

        @pl.when(k == 0)
        def _():
            from_own()
            loads[8].wait()
            loads[9].wait()

        for b in range(5):
            put_trace(0, b, xs[k, b, 0:16])
            put_trace(1, b, xs[k, b, 48:64])
            for f in range(4):
                put_trace(2 + f, b, traces[k, f, b])
        gathered = jnp.dot(
            gather_left[:, 0:768], pick_own[...], preferred_element_type=F32
        )
        rows[0] = gathered[0:80] + gathered[80:160]

        @pl.loop(0, 4)
        def _(c):
            chunk = pl.ds(pl.multiple_of(16 * c, 16), 16)
            total = [
                (diagonal[a, chunk].astype(F32) - SHIFT) * xs[k, a, chunk] for a in range(5)
            ]
            for d in range(3):
                for b in range(5):
                    slope = slopes[
                        pl.ds(pl.multiple_of(64 * d + 16 * c, 16), 16),
                        b * LANES : (b + 1) * LANES,
                    ]
                    for a in range(5):
                        total[a] = total[a] + volume[d, a, b, chunk].astype(F32) * slope
            for a in range(5):
                xs[k + 1, a, chunk] = total[a]

        products(k, k + 1)

        @pl.when(k == 0)
        def _():
            from_neighbours()
            loads[10].wait()
            loads[11].wait()

        arrive(0, k)
        for s in range(2):
            for b in range(5):
                put_trace(6 + s, b, halo_x[k, s, b])
        gathered = jnp.dot(
            gather_left[:, 768:1024], pick_halo[...], preferred_element_type=F32
        )
        gathered = gathered[0:80] + gathered[80:160]
        rows[0] = rows[0] + gathered[:, 0:128]
        rows[1] = gathered[:, 128:256]
        for g in range(2):
            before = [rows[g, 16 * b : 16 * b + 16] for b in range(5)]
            for a in range(5):
                value = coupling[g, 5 * a : 5 * a + 1] * before[0]
                for b in range(1, 5):
                    row = 5 * a + b
                    value = value + coupling[g, row : row + 1] * before[b]
                rows[g, 16 * a : 16 * a + 16] = value
            nodes = [rows[g, pl.ds(m, 5, stride=16), :] for m in range(16)]
            for stage in range(2):
                after = [None] * 16
                for i in range(4):
                    for j in range(4):
                        own_index = i if stage == 0 else j
                        for m in range(4):
                            row = 16 * stage + 4 * own_index + m
                            node = 4 * m + j if stage == 0 else 4 * i + m
                            term = maps[g, row : row + 1] * nodes[node]
                            at = 4 * i + j
                            after[at] = term if m == 0 else after[at] + term
                nodes = after
            for m in range(16):
                rows[g, pl.ds(m, 5, stride=16), :] = nodes[m]
            high, low = split(rows[g])
            rows_left[0:80, g * LANES : (g + 1) * LANES] = high
            rows_left[80:160, g * LANES : (g + 1) * LANES] = low
        faces[...] = lax.dot_general(
            rows_left[...], place[...], (((1,), (1,)), ((), ())), preferred_element_type=F32
        )
        arrive(1, k)
        arrive(2, k)
        for f in range(6):
            d, s = f // 2, f % 2
            if d == 0:
                beside = [halo_x[k, s, b] for b in range(5)]
            elif d == 1:
                beside = [halo_y[k, s, b] for b in range(5)]
            else:
                edge = lane == (LANES - 1 if s == 0 else 0)
                turn = 1 if s == 0 else LANES - 1
                beside = [
                    pltpu.roll(
                        jnp.where(edge, halo_z[k, s, b], traces[k, 3 - s, b]), turn, 1
                    )
                    for b in range(5)
                ]
            columns = slice(f * LANES, (f + 1) * LANES)
            for a in range(5):
                value = (
                    faces[16 * a : 16 * a + 16, columns]
                    + faces[80 + 16 * a : 96 + 16 * a, columns]
                )
                for b in range(5):
                    value = value + surface[f, a, b].astype(F32) * beside[b]
                if d == 0:
                    at = 48 * s
                    xs[k + 1, a, at : at + 16] = xs[k + 1, a, at : at + 16] + value
                else:
                    high, low = split(value)
                    at = 16 * (f - 2)
                    faces_left[at : at + 16, a * LANES : (a + 1) * LANES] = high
                    faces_left[64 + at : 80 + at, a * LANES : (a + 1) * LANES] = low
        added = jnp.dot(back[...], faces_left[...], preferred_element_type=F32)
        for a in range(5):
            xs[k + 1, a] = xs[k + 1, a] + added[:, a * LANES : (a + 1) * LANES]

    last = [jnp.zeros((8, LANES), F32)] * (KRYLOV + 1)
    for b in range(5):
        for r in range(8):
            at = slice(8 * r, 8 * r + 8)
            newest = xs[KRYLOV, b, at]
            for i in range(KRYLOV):
                last[i] = last[i] + newest * xs[i, b, at]
            last[KRYLOV] = last[KRYLOV] + newest * newest
    for i in range(KRYLOV + 1):
        row = KRYLOV * 8 + i
        gram[row : row + 1] = jnp.sum(last[i], axis=0, keepdims=True)
    sums = lax.dot_general(
        jnp.ones((8, LANES), F32),
        gram[...],
        (((1,), (1,)), ((), ())),
        preferred_element_type=F32,
        precision=lax.Precision.HIGHEST,
    )
    message[...] = sums[0:1]

    def sum_copy(step):
        return pltpu.make_async_remote_copy(
            src_ref=message,
            dst_ref=messages.at[step],
            send_sem=sum_send.at[step],
            recv_sem=sum_recv.at[step],
            device_id=peer(step),
            device_id_type=MESH,
        )

    each(lambda step: sum_copy(step).start())
    messages[0] = message[...]
    each(lambda step: sum_copy(step).wait_recv())
    total = jnp.sum(messages[...], axis=0)
    size = KRYLOV + 1
    entries = [[None] * size for _ in range(size)]
    for k in range(size):
        for i in range(k + 1):
            entry = jnp.sum(jnp.where(lane == 8 * k + i, total, 0.0), axis=1, keepdims=True)
            entry = jnp.broadcast_to(entry, (8, LANES))
            entries[k][i] = entries[i][k] = entry
    scales = small_solve(entries)
    for b in range(5):
        for r in range(8):
            at = slice(8 * r, 8 * r + 8)
            value = scales[0] * xs[0, b, at]
            for k in range(1, KRYLOV):
                value = value + scales[k] * xs[k, b, at]
            out[b, at] = value

    each(lambda step: sum_copy(step).wait_send())


def local(
    sizes,
    adjoint_source,
    diagonal,
    volume_coupling,
    surface_coupling,
    mortar_owner,
    mortar_fine,
    mortar_coarse,
    mortar_quarter,
    mortar_side,
    mortar_coupling,
):
    forward, back = node_matrices()
    count = mortar_fine.shape[0]
    pairs = mortar_coupling.transpose(2, 3, 1, 0).reshape(25, 2, count)
    group = sizes[0] * sizes[1] * sizes[2]
    vmem = pl.BlockSpec(memory_space=pltpu.VMEM)
    dma = pltpu.SemaphoreType.DMA
    result = pl.pallas_call(
        functools.partial(kernel, sizes),
        out_shape=jax.ShapeDtypeStruct((5, 64, LANES), F32),
        in_specs=[pl.BlockSpec(memory_space=pltpu.HBM)] * 12,
        out_specs=vmem,
        scratch_shapes=[
            pltpu.VMEM((5, 64, LANES), BF16),
            pltpu.VMEM((3, 5, 5, 64, LANES), BF16),
            pltpu.VMEM((6, 5, 5, 16, LANES), BF16),
            pltpu.VMEM((5, 1, 64), jnp.int32),
            pltpu.VMEM((25, 2, 64), F32),
            pltpu.VMEM((192, 256), BF16),
            pltpu.VMEM((64, 128), BF16),
            pltpu.VMEM((32, LANES), F32),
            dma((12,)),
            pltpu.VMEM((KRYLOV + 1, 5, 64, LANES), F32),
            pltpu.VMEM((192, 5 * LANES), F32),
            pltpu.VMEM((256, 5 * LANES), BF16),
            pltpu.VMEM((KRYLOV, 4, 5, 16, LANES), F32),
            pltpu.VMEM((KRYLOV, 2, 5, 16, LANES), F32),
            pltpu.VMEM((KRYLOV, 2, 5, 16, LANES), F32),
            pltpu.VMEM((KRYLOV, 2, 5, 16, LANES), F32),
            pltpu.VMEM((2, 32, LANES), F32),
            pltpu.VMEM((160, 8 * LANES), BF16),
            pltpu.VMEM((6 * LANES, LANES), BF16),
            pltpu.VMEM((2 * LANES, 2 * LANES), BF16),
            pltpu.VMEM((6 * LANES, 2 * LANES), BF16),
            pltpu.VMEM((2, 32, LANES), F32),
            pltpu.VMEM((2, 32, LANES), F32),
            pltpu.VMEM((2, 80, LANES), F32),
            pltpu.VMEM((160, 2 * LANES), BF16),
            pltpu.VMEM((160, 6 * LANES), F32),
            pltpu.VMEM((128, 5 * LANES), BF16),
            pltpu.VMEM((LANES, LANES), F32),
            pltpu.VMEM((1, LANES), F32),
            pltpu.VMEM((group, 1, LANES), F32),
            dma((KRYLOV, 3, 2)),
            dma((KRYLOV, 3, 2)),
            dma((2,)),
            dma((2,)),
            dma((group,)),
            dma((group,)),
        ],
        compiler_params=pltpu.CompilerParams(
            collective_id=0, has_side_effects=True, vmem_limit_bytes=63 * 1024 * 1024
        ),
    )(
        adjoint_source.reshape(5, 64, LANES),
        diagonal.reshape(5, 64, LANES),
        volume_coupling.reshape(3, 5, 5, 64, LANES),
        surface_coupling.reshape(6, 5, 5, 16, LANES),
        mortar_owner.reshape(1, count),
        mortar_fine.reshape(1, count),
        mortar_coarse.reshape(1, count),
        mortar_quarter.reshape(1, count),
        mortar_side.reshape(1, count),
        pairs,
        jnp.asarray(forward),
        jnp.asarray(back),
    )
    return result.reshape(adjoint_source.shape)


def solution(mesh):
    placed = (
        P(None, None, None, None, ("groups", "gx"), "gy", "gz"),
        P(None, None, None, None, ("groups", "gx"), "gy", "gz"),
        P(None, None, None, None, None, None, ("groups", "gx"), "gy", "gz"),
        P(None, None, None, None, None, ("groups", "gx"), "gy", "gz"),
        P(("groups", "gx", "gy", "gz"), None),
        P(("groups", "gx", "gy", "gz")),
        P(("groups", "gx", "gy", "gz")),
        P(("groups", "gx", "gy", "gz")),
        P(("groups", "gx", "gy", "gz")),
        P(("groups", "gx", "gy", "gz"), None, None, None),
    )
    sizes = tuple(mesh.shape[a] for a in ("gx", "gy", "gz"))
    return jax.shard_map(
        functools.partial(local, sizes),
        mesh=mesh,
        in_specs=placed,
        out_specs=P(None, None, None, None, ("groups", "gx"), "gy", "gz"),
        check_vma=False,
    )
```

```python
import functools

import jax
import jax.numpy as jnp
import ml_dtypes
import numpy as np
from jax import lax
from jax.experimental import pallas as pl
from jax.experimental.pallas import tpu as pltpu
from jax.sharding import PartitionSpec as P

KRYLOV = 4
SHIFT = 3.0
F32 = jnp.float32
BF16 = jnp.bfloat16
LANES = 128
MESH = pl.DeviceIdType.MESH


def node_tables():
    points = np.array([-1.0, -1.0 / np.sqrt(5.0), 1.0 / np.sqrt(5.0), 1.0])
    barycentric = np.array(
        [1.0 / np.prod([points[m] - points[k] for k in range(4) if k != m]) for m in range(4)]
    )
    derivative = np.zeros((4, 4))
    for i in range(4):
        for m in range(4):
            if i != m:
                derivative[i, m] = barycentric[m] / barycentric[i] / (points[i] - points[m])
    for i in range(4):
        derivative[i, i] = -np.sum(derivative[i])
    halves = []
    for h in range(2):
        shifted = (points + 2 * h - 1) / 2.0
        lagrange = np.ones((4, 4))
        for m in range(4):
            for k in range(4):
                if k != m:
                    lagrange[:, m] = (
                        lagrange[:, m] * (shifted - points[k]) / (points[m] - points[k])
                    )
        halves.append(lagrange)
    return derivative.astype(np.float32), np.stack(halves).astype(np.float32)


def split(value):
    high = value.astype(BF16)
    return high, (value - high.astype(F32)).astype(BF16)


def node_matrices():
    derivative, _ = node_tables()
    eye = np.eye(4, dtype=np.float32)
    slopes = [
        np.kron(np.kron(derivative.T, eye), eye),
        np.kron(np.kron(eye, derivative.T), eye),
        np.kron(np.kron(eye, eye), derivative.T),
    ]
    traces = []
    for node in (0, 3):
        traces.append(np.kron(np.kron(eye, eye[node : node + 1]), eye))
    for node in (0, 3):
        traces.append(np.kron(np.kron(eye, eye), eye[node : node + 1]))
    traces = np.concatenate(traces)
    rows = np.concatenate(slopes)
    high = rows.astype(ml_dtypes.bfloat16)
    low = (rows - high.astype(np.float32)).astype(ml_dtypes.bfloat16)
    forward = np.concatenate([high, high, low, low], axis=1)
    back = np.concatenate([traces.T, traces.T], axis=1).astype(ml_dtypes.bfloat16)
    return forward, back


def small_solve(gram):
    size = KRYLOV + 1
    norm = jnp.sqrt(gram[0][0] + 1e-6)
    one = jnp.ones_like(norm)
    basis = [[one / norm]]
    images = [[gram[0][i] / norm for i in range(size)]]
    hess = [[None] * KRYLOV for _ in range(size)]
    for column in range(KRYLOV):
        current = basis[column]
        mapped = [SHIFT * c for c in current] + [None]
        for i, c in enumerate(current):
            mapped[i + 1] = c if mapped[i + 1] is None else mapped[i + 1] + c
        for earlier in range(column + 1):
            product = sum(m * images[earlier][i] for i, m in enumerate(mapped))
            hess[earlier][column] = product
            for i, c in enumerate(basis[earlier]):
                mapped[i] = mapped[i] - product * c
        image = [sum(m * gram[k][i] for k, m in enumerate(mapped)) for i in range(size)]
        square = sum(m * image[i] for i, m in enumerate(mapped))
        length = jnp.sqrt(jnp.maximum(square, 0.0) + 1e-6)
        hess[column + 1][column] = length
        if column + 1 < KRYLOV:
            scale = one / length
            basis.append([m * scale for m in mapped])
            images.append([m * scale for m in image])
    normal = [[None] * KRYLOV for _ in range(KRYLOV)]
    for i in range(KRYLOV):
        for j in range(i + 1):
            normal[i][j] = sum(hess[r][i] * hess[r][j] for r in range(j + 2))
    factor = [[None] * KRYLOV for _ in range(KRYLOV)]
    inverse = [None] * KRYLOV
    for j in range(KRYLOV):
        pivot = normal[j][j]
        for k in range(j):
            pivot = pivot - factor[j][k] * factor[j][k]
        factor[j][j] = jnp.sqrt(pivot)
        inverse[j] = one / factor[j][j]
        for i in range(j + 1, KRYLOV):
            value = normal[i][j]
            for k in range(j):
                value = value - factor[i][k] * factor[j][k]
            factor[i][j] = value * inverse[j]
    half = []
    for i in range(KRYLOV):
        value = norm * hess[0][i]
        for k in range(i):
            value = value - factor[i][k] * half[k]
        half.append(value * inverse[i])
    weights = [None] * KRYLOV
    for i in reversed(range(KRYLOV)):
        value = half[i]
        for k in range(i + 1, KRYLOV):
            value = value - factor[k][i] * weights[k]
        weights[i] = value * inverse[i]
    return [
        sum(weights[j] * basis[j][i] for j in range(i, KRYLOV)) for i in range(KRYLOV)
    ]


def kernel(
    sizes,
    source_hbm,
    diagonal_hbm,
    volume_hbm,
    surface_hbm,
    owner_hbm,
    fine_hbm,
    coarse_hbm,
    quarter_hbm,
    side_hbm,
    coupling_hbm,
    forward_hbm,
    back_hbm,
    out,
    diagonal,
    volume,
    surface,
    numbers,
    pairs,
    forward,
    back,
    pack,
    load_sem,
    xs,
    slopes,
    right,
    traces,
    halo_x,
    halo_y,
    halo_z,
    neighbour_pack,
    gather_left,
    pick_own,
    pick_halo,
    place,
    coupling,
    maps,
    rows,
    rows_left,
    faces,
    faces_left,
    gram,
    message,
    messages,
    send_sem,
    recv_sem,
    pack_send,
    pack_recv,
    sum_send,
    sum_recv,
):
    axes = ("gx", "gy", "gz")
    here = [lax.axis_index(a) for a in axes]
    group = sizes[0] * sizes[1] * sizes[2]
    me = (here[0] * sizes[1] + here[1]) * sizes[2] + here[2]
    has_low = [h > 0 for h in here]
    has_high = [h < n - 1 for h, n in zip(here, sizes)]

    def wrapped(value, size):
        return jnp.where(value >= size, value - size, value)

    def each(action):
        if group > 16:
            pl.loop(1, group)(action)
        else:
            for step in range(1, group):
                action(step)

    def peer(step):
        if isinstance(step, int):
            steps = (step // (sizes[1] * sizes[2]), step // sizes[2] % sizes[1], step % sizes[2])
            return {a: wrapped(h + o, n) for a, h, o, n in zip(axes, here, steps, sizes)}
        other = lax.rem(me + step, group)
        return {
            "gx": other // (sizes[1] * sizes[2]),
            "gy": lax.rem(other // sizes[2], sizes[1]),
            "gz": lax.rem(other, sizes[2]),
        }

    barrier = pltpu.get_barrier_semaphore()

    each(
        lambda step: pl.semaphore_signal(
            barrier, inc=1, device_id=peer(step), device_id_type=MESH
        )
    )

    loads = [
        pltpu.make_async_copy(origin, target, load_sem.at[i])
        for i, (origin, target) in enumerate(
            (
                (source_hbm, xs.at[0]),
                (owner_hbm, numbers.at[0]),
                (fine_hbm, numbers.at[1]),
                (coarse_hbm, numbers.at[2]),
                (quarter_hbm, numbers.at[3]),
                (side_hbm, numbers.at[4]),
                (coupling_hbm, pairs),
                (forward_hbm, forward),
                (diagonal_hbm, diagonal),
                (volume_hbm, volume),
                (surface_hbm, surface),
                (back_hbm, back),
            )
        )
    ]
    for load in loads:
        load.start()

    halos = (halo_x, halo_y, halo_z)
    for d in range(3):
        for s, there in ((0, has_low[d]), (1, has_high[d])):

            @pl.when(jnp.logical_not(there))
            def _(d=d, s=s):
                for k in range(KRYLOV):
                    halos[d][k, s] = jnp.zeros((5, 16, LANES), F32)

                if d == 0:
                    neighbour_pack[s] = jnp.full((32, LANES), -9.0, F32)

    pl.semaphore_wait(barrier, group - 1)

    def to(d, s):
        return {axes[d]: here[d] - 1 if s == 0 else here[d] + 1}

    def pack_copy(s):
        return pltpu.make_async_remote_copy(
            src_ref=pack,
            dst_ref=neighbour_pack.at[1 - s],
            send_sem=pack_send.at[s],
            recv_sem=pack_recv.at[s],
            device_id=to(0, s),
            device_id_type=MESH,
        )

    def face_copy(d, s, k):
        if d == 0:
            face = xs.at[k, :, pl.ds(48 * s, 16), :]
        else:
            face = traces.at[k, 2 * (d - 1) + s]
        return pltpu.make_async_remote_copy(
            src_ref=face,
            dst_ref=halos[d].at[k, 1 - s],
            send_sem=send_sem.at[k, d, s],
            recv_sem=recv_sem.at[k, d, s],
            device_id=to(d, s),
            device_id_type=MESH,
        )

    def sides(d, s):
        return (has_low[d], has_high[d]) if s == 0 else (has_high[d], has_low[d])

    def start(d, k):
        for s in range(2):
            target, _ = sides(d, s)

            @pl.when(target)
            def _(s=s):
                face_copy(d, s, k).start()

    def arrive(d, k):
        for s in range(2):
            target, origin = sides(d, s)

            @pl.when(origin)
            def _(s=s):
                face_copy(d, s, k).wait_recv()

            @pl.when(target)
            def _(s=s):
                face_copy(d, s, k).wait_send()

    loads[0].wait()
    start(0, 0)
    for load in loads[1:7]:
        load.wait()
    for half in range(2):
        at = slice(64 * half, 64 * half + 64)
        pack[0:25, at] = pairs[:, half, :]
        for i in range(5):
            pack[25 + i : 26 + i, at] = numbers[i].astype(F32)
    pack[30:32] = jnp.zeros((2, LANES), F32)
    for s in range(2):

        @pl.when(sides(0, s)[0])
        def _(s=s):
            pack_copy(s).start()

    lane = lax.broadcasted_iota(jnp.int32, (1, LANES), 1)
    left_half = lane < 64
    _, halves = node_tables()

    def keys(packed, me_x):
        offset = packed[25:26] - me_x
        fine, coarse, quarter, side = (packed[r : r + 1] for r in range(26, 30))
        odd = jnp.floor(side * 0.5)
        opposite = side + 1.0 - 2.0 * (side - 2.0 * odd)
        return offset, fine, coarse, quarter, side, opposite

    def one_hot(key, count):
        index = lax.broadcasted_iota(jnp.int32, (count, LANES), 0).astype(F32)
        return jnp.where(index == key, 1.0, 0.0).astype(BF16)

    def make_maps(slot, quarter, flipped):
        first = quarter >= 2.0
        second = (quarter - 2.0 * jnp.where(first, 1.0, 0.0)) >= 1.0
        for stage, bit in ((0, first), (1, second)):
            for i in range(4):
                for m in range(4):
                    straight = jnp.where(bit, float(halves[1, i, m]), float(halves[0, i, m]))
                    turned = jnp.where(bit, float(halves[1, m, i]), float(halves[0, m, i]))
                    row = 16 * stage + 4 * i + m
                    maps[slot, row : row + 1] = jnp.where(flipped, turned, straight)

    place_x = here[0].astype(F32)

    def from_own():
        own = pack[...]
        offset, fine, coarse, quarter, side, opposite = keys(own, place_x)
        same = offset == 0.0
        at_coarse = jnp.where(same, opposite * LANES + coarse, -1.0)
        at_fine = side * LANES + fine
        pick_own[...] = one_hot(
            jnp.where(left_half, at_coarse, jnp.where(same, at_fine, -1.0)), 768
        )
        outside = jnp.where(offset < 0.0, coarse, LANES + coarse)
        pick_halo[:, 0:128] = one_hot(
            jnp.where(left_half & jnp.logical_not(same), outside, -1.0), 256
        )
        place[:, 0:128] = one_hot(jnp.where(left_half, at_fine, at_coarse), 768)
        coupling[0] = own
        make_maps(0, quarter, jnp.logical_not(left_half))

    def from_neighbours():
        for s in range(2):
            target, origin = sides(0, s)

            @pl.when(origin)
            def _(s=s):
                pack_copy(s).wait_recv()

            @pl.when(target)
            def _(s=s):
                pack_copy(s).wait_send()

        both = jnp.where(left_half, pltpu.roll(neighbour_pack[0], 64, 1), neighbour_pack[1])
        offset, fine, coarse, quarter, _, _ = keys(both, place_x)
        valid = offset == 0.0
        base = jnp.where(left_half, 0.0, 1.0 * LANES)
        pick_halo[:, 128:256] = one_hot(jnp.where(valid, base + fine, -1.0), 256)
        place[:, 128:256] = one_hot(jnp.where(valid, base + coarse, -1.0), 768)
        coupling[1] = jnp.where(valid, both, 0.0)
        make_maps(1, jnp.where(valid, quarter, 0.0), lane >= 0)

    def put_trace(block, var, value):
        high, low = split(value)
        columns = pl.ds(block * LANES, LANES)
        gather_left[pl.ds(16 * var, 16), columns] = high
        gather_left[pl.ds(80 + 16 * var, 16), columns] = low

    def products(k, count):
        @pl.loop(0, count)
        def _(i):
            total = jnp.zeros((8, LANES), F32)
            for b in range(5):
                both = xs[k, b] * xs[i, b]
                for r in range(8):
                    total = total + both[8 * r : 8 * r + 8]
            gram[pl.ds(k * 8 + i, 1), :] = jnp.sum(total, axis=0, keepdims=True)

    gram[...] = jnp.zeros_like(gram)

    @pl.loop(0, KRYLOV)
    def _(k):

        @pl.when(k > 0)
        def _():
            start(0, k)

        for s in range(2):
            for b in range(5):
                for i in range(4):
                    at = 16 * i + 12 * s
                    traces[k, s, b, 4 * i : 4 * i + 4] = xs[k, b, at : at + 4]
        start(1, k)
        for s in range(2):
            for b in range(5):
                traces[k, 2 + s, b] = xs[k, b, pl.ds(3 * s, 16, stride=4), :]
        start(2, k)
        for b in range(5):
            high, low = split(xs[k, b])
            columns = slice(b * LANES, (b + 1) * LANES)
            right[0:64, columns] = high
            right[64:128, columns] = low
            right[128:192, columns] = high
            right[192:256, columns] = low

        @pl.when(k == 0)
        def _():
            loads[7].wait()

        slopes[...] = jnp.dot(forward[...], right[...], preferred_element_type=F32)

        @pl.when(k == 0)
        def _():
            from_own()
            loads[8].wait()
            loads[9].wait()

        for b in range(5):
            put_trace(0, b, xs[k, b, 0:16])
            put_trace(1, b, xs[k, b, 48:64])
            for f in range(4):
                put_trace(2 + f, b, traces[k, f, b])
        gathered = jnp.dot(
            gather_left[:, 0:768], pick_own[...], preferred_element_type=F32
        )
        rows[0] = gathered[0:80] + gathered[80:160]

        @pl.loop(0, 4)
        def _(c):
            chunk = pl.ds(pl.multiple_of(16 * c, 16), 16)
            total = [
                (diagonal[a, chunk].astype(F32) - SHIFT) * xs[k, a, chunk] for a in range(5)
            ]
            for d in range(3):
                for b in range(5):
                    slope = slopes[
                        pl.ds(pl.multiple_of(64 * d + 16 * c, 16), 16),
                        b * LANES : (b + 1) * LANES,
                    ]
                    for a in range(5):
                        total[a] = total[a] + volume[d, a, b, chunk].astype(F32) * slope
            for a in range(5):
                xs[k + 1, a, chunk] = total[a]

        products(k, k + 1)

        @pl.when(k == 0)
        def _():
            from_neighbours()
            loads[10].wait()
            loads[11].wait()

        arrive(0, k)
        for s in range(2):
            for b in range(5):
                put_trace(6 + s, b, halo_x[k, s, b])
        gathered = jnp.dot(
            gather_left[:, 768:1024], pick_halo[...], preferred_element_type=F32
        )
        gathered = gathered[0:80] + gathered[80:160]
        rows[0] = rows[0] + gathered[:, 0:128]
        rows[1] = gathered[:, 128:256]
        for g in range(2):
            before = [rows[g, 16 * b : 16 * b + 16] for b in range(5)]
            for a in range(5):
                value = coupling[g, 5 * a : 5 * a + 1] * before[0]
                for b in range(1, 5):
                    row = 5 * a + b
                    value = value + coupling[g, row : row + 1] * before[b]
                rows[g, 16 * a : 16 * a + 16] = value
            nodes = [rows[g, pl.ds(m, 5, stride=16), :] for m in range(16)]
            for stage in range(2):
                after = [None] * 16
                for i in range(4):
                    for j in range(4):
                        own_index = i if stage == 0 else j
                        for m in range(4):
                            row = 16 * stage + 4 * own_index + m
                            node = 4 * m + j if stage == 0 else 4 * i + m
                            term = maps[g, row : row + 1] * nodes[node]
                            at = 4 * i + j
                            after[at] = term if m == 0 else after[at] + term
                nodes = after
            for m in range(16):
                rows[g, pl.ds(m, 5, stride=16), :] = nodes[m]
            high, low = split(rows[g])
            rows_left[0:80, g * LANES : (g + 1) * LANES] = high
            rows_left[80:160, g * LANES : (g + 1) * LANES] = low
        faces[...] = lax.dot_general(
            rows_left[...], place[...], (((1,), (1,)), ((), ())), preferred_element_type=F32
        )
        arrive(1, k)
        arrive(2, k)
        for f in range(6):
            d, s = f // 2, f % 2
            if d == 0:
                beside = [halo_x[k, s, b] for b in range(5)]
            elif d == 1:
                beside = [halo_y[k, s, b] for b in range(5)]
            else:
                edge = lane == (LANES - 1 if s == 0 else 0)
                turn = 1 if s == 0 else LANES - 1
                beside = [
                    pltpu.roll(
                        jnp.where(edge, halo_z[k, s, b], traces[k, 3 - s, b]), turn, 1
                    )
                    for b in range(5)
                ]
            columns = slice(f * LANES, (f + 1) * LANES)
            for a in range(5):
                value = (
                    faces[16 * a : 16 * a + 16, columns]
                    + faces[80 + 16 * a : 96 + 16 * a, columns]
                )
                for b in range(5):
                    value = value + surface[f, a, b].astype(F32) * beside[b]
                if d == 0:
                    at = 48 * s
                    xs[k + 1, a, at : at + 16] = xs[k + 1, a, at : at + 16] + value
                else:
                    high, low = split(value)
                    at = 16 * (f - 2)
                    faces_left[at : at + 16, a * LANES : (a + 1) * LANES] = high
                    faces_left[64 + at : 80 + at, a * LANES : (a + 1) * LANES] = low
        added = jnp.dot(back[...], faces_left[...], preferred_element_type=F32)
        for a in range(5):
            xs[k + 1, a] = xs[k + 1, a] + added[:, a * LANES : (a + 1) * LANES]

    last = [jnp.zeros((8, LANES), F32)] * (KRYLOV + 1)
    for b in range(5):
        for r in range(8):
            at = slice(8 * r, 8 * r + 8)
            newest = xs[KRYLOV, b, at]
            for i in range(KRYLOV):
                last[i] = last[i] + newest * xs[i, b, at]
            last[KRYLOV] = last[KRYLOV] + newest * newest
    for i in range(KRYLOV + 1):
        row = KRYLOV * 8 + i
        gram[row : row + 1] = jnp.sum(last[i], axis=0, keepdims=True)
    sums = lax.dot_general(
        jnp.ones((8, LANES), F32),
        gram[...],
        (((1,), (1,)), ((), ())),
        preferred_element_type=F32,
        precision=lax.Precision.HIGHEST,
    )
    message[...] = sums[0:1]

    def sum_copy(step):
        return pltpu.make_async_remote_copy(
            src_ref=message,
            dst_ref=messages.at[step],
            send_sem=sum_send.at[step],
            recv_sem=sum_recv.at[step],
            device_id=peer(step),
            device_id_type=MESH,
        )

    each(lambda step: sum_copy(step).start())
    messages[0] = message[...]
    each(lambda step: sum_copy(step).wait_recv())
    total = jnp.sum(messages[...], axis=0)
    size = KRYLOV + 1
    entries = [[None] * size for _ in range(size)]
    for k in range(size):
        for i in range(k + 1):
            entry = jnp.sum(jnp.where(lane == 8 * k + i, total, 0.0), axis=1, keepdims=True)
            entry = jnp.broadcast_to(entry, (8, LANES))
            entries[k][i] = entries[i][k] = entry
    scales = small_solve(entries)
    for b in range(5):
        for r in range(8):
            at = slice(8 * r, 8 * r + 8)
            value = scales[0] * xs[0, b, at]
            for k in range(1, KRYLOV):
                value = value + scales[k] * xs[k, b, at]
            out[b, at] = value

    each(lambda step: sum_copy(step).wait_send())


def local(
    sizes,
    adjoint_source,
    diagonal,
    volume_coupling,
    surface_coupling,
    mortar_owner,
    mortar_fine,
    mortar_coarse,
    mortar_quarter,
    mortar_side,
    mortar_coupling,
):
    forward, back = node_matrices()
    count = mortar_fine.shape[0]
    pairs = mortar_coupling.transpose(2, 3, 1, 0).reshape(25, 2, count)
    group = sizes[0] * sizes[1] * sizes[2]
    vmem = pl.BlockSpec(memory_space=pltpu.VMEM)
    dma = pltpu.SemaphoreType.DMA
    result = pl.pallas_call(
        functools.partial(kernel, sizes),
        out_shape=jax.ShapeDtypeStruct((5, 64, LANES), F32),
        in_specs=[pl.BlockSpec(memory_space=pltpu.HBM)] * 12,
        out_specs=vmem,
        scratch_shapes=[
            pltpu.VMEM((5, 64, LANES), BF16),
            pltpu.VMEM((3, 5, 5, 64, LANES), BF16),
            pltpu.VMEM((6, 5, 5, 16, LANES), BF16),
            pltpu.VMEM((5, 1, 64), jnp.int32),
            pltpu.VMEM((25, 2, 64), F32),
            pltpu.VMEM((192, 256), BF16),
            pltpu.VMEM((64, 128), BF16),
            pltpu.VMEM((32, LANES), F32),
            dma((12,)),
            pltpu.VMEM((KRYLOV + 1, 5, 64, LANES), F32),
            pltpu.VMEM((192, 5 * LANES), F32),
            pltpu.VMEM((256, 5 * LANES), BF16),
            pltpu.VMEM((KRYLOV, 4, 5, 16, LANES), F32),
            pltpu.VMEM((KRYLOV, 2, 5, 16, LANES), F32),
            pltpu.VMEM((KRYLOV, 2, 5, 16, LANES), F32),
            pltpu.VMEM((KRYLOV, 2, 5, 16, LANES), F32),
            pltpu.VMEM((2, 32, LANES), F32),
            pltpu.VMEM((160, 8 * LANES), BF16),
            pltpu.VMEM((6 * LANES, LANES), BF16),
            pltpu.VMEM((2 * LANES, 2 * LANES), BF16),
            pltpu.VMEM((6 * LANES, 2 * LANES), BF16),
            pltpu.VMEM((2, 32, LANES), F32),
            pltpu.VMEM((2, 32, LANES), F32),
            pltpu.VMEM((2, 80, LANES), F32),
            pltpu.VMEM((160, 2 * LANES), BF16),
            pltpu.VMEM((160, 6 * LANES), F32),
            pltpu.VMEM((128, 5 * LANES), BF16),
            pltpu.VMEM((LANES, LANES), F32),
            pltpu.VMEM((1, LANES), F32),
            pltpu.VMEM((group, 1, LANES), F32),
            dma((KRYLOV, 3, 2)),
            dma((KRYLOV, 3, 2)),
            dma((2,)),
            dma((2,)),
            dma((group,)),
            dma((group,)),
        ],
        compiler_params=pltpu.CompilerParams(
            collective_id=0, has_side_effects=True, vmem_limit_bytes=63 * 1024 * 1024
        ),
    )(
        adjoint_source.reshape(5, 64, LANES),
        diagonal.reshape(5, 64, LANES),
        volume_coupling.reshape(3, 5, 5, 64, LANES),
        surface_coupling.reshape(6, 5, 5, 16, LANES),
        mortar_owner.reshape(1, count),
        mortar_fine.reshape(1, count),
        mortar_coarse.reshape(1, count),
        mortar_quarter.reshape(1, count),
        mortar_side.reshape(1, count),
        pairs,
        jnp.asarray(forward),
        jnp.asarray(back),
    )
    return result.reshape(adjoint_source.shape)


def solution(mesh):
    placed = (
        P(None, None, None, None, ("groups", "gx"), "gy", "gz"),
        P(None, None, None, None, ("groups", "gx"), "gy", "gz"),
        P(None, None, None, None, None, None, ("groups", "gx"), "gy", "gz"),
        P(None, None, None, None, None, ("groups", "gx"), "gy", "gz"),
        P(("groups", "gx", "gy", "gz"), None),
        P(("groups", "gx", "gy", "gz")),
        P(("groups", "gx", "gy", "gz")),
        P(("groups", "gx", "gy", "gz")),
        P(("groups", "gx", "gy", "gz")),
        P(("groups", "gx", "gy", "gz"), None, None, None),
    )
    sizes = tuple(mesh.shape[a] for a in ("gx", "gy", "gz"))
    return jax.shard_map(
        functools.partial(local, sizes),
        mesh=mesh,
        in_specs=placed,
        out_specs=P(None, None, None, None, ("groups", "gx"), "gy", "gz"),
        check_vma=False,
    )
```
